32 devices in a mesh: fine: 8 (over z, y), tele: 4 (over x, core).
Axes of the slice: x: 2, y: 2, z: 4, core: 2. Of those that a mesh axis runs over, the one named last changes fastest.
Arguments:
- right_side: float32 [512, 320], P(('fine', 'tele')), may hold values from -6 to 6
- fine_inverse: bfloat16 [512, 320, 320], P(('fine', 'tele')), may hold values from -0.08 to 0.45
- fine_links: int32 [512, 6], P(('fine', 'tele')), may hold values from -1 to 511, as said below
- fine_faces: int32 [512, 6], P(('fine', 'tele')), may hold values from 0 to 23
- coarse_inverse: bfloat16 [64, 320, 320], P(('fine', 'tele')), may hold values from -0.04 to 0.21
- coarse_links: int32 [64, 6], P(('fine', 'tele')), may hold values from -1 to 63, as said below
- coarse_faces: int32 [64, 6], P(('fine', 'tele')), may hold values from 0 to 23
- face_operators: bfloat16 [24, 80, 80], replicated, may hold values from -1.25 to 1.25
- agglomerate: int32 [512], P(('fine', 'tele')), may hold values from 0 to 63, as said below
Outputs:
- solution: float32 [512, 320], P(('fine', 'tele'))
The draws below stay inside these ranges and needn't reach their ends.
Inputs may be any that keep to these rules, and one draw needn't show every extreme that they name: `fine_links`: any entry other than -1 is an element held by the same device as the element, or by the device just before or after it in the order of fine+tele, cyclically. `coarse_links`: coarse elements form blocks of 8 consecutive ones; any entry other than -1 lies in the element's own block or in the block just before or after it, cyclically. `agglomerate`: fine element i maps into block i // 64 of 8 consecutive coarse elements; every coarse element collects exactly 8 fine elements.
All inputs are finite; a program needn't handle non-finite values.
Results may differ from the reference program's by a relative error of at most 0.02.
Values may be sent and summed in bfloat16 or wider, within the bound.
A program may use at most 64 MiB of HBM per device.

```python
import math
import jax
import jax.numpy as jnp
from jax import lax

FIELDS = 5
NODES = 4
BLOCK_DOFS = 320
FACE_DOFS = 80
FACE_TYPES = 24
E_DEV = 16
AGGLOMERATE = 8
SWEEPS = 3
CYCLES = 2
COLUMN = 8
FINE_COLUMN = 64
ELEMENTS = 512
COARSE = 64


def inverse_blocks(key, row_count, low_diag, high_diag, off_scale):
    key_diag, key_off = jax.random.split(key)
    shape = (row_count, BLOCK_DOFS, BLOCK_DOFS)
    diagonal = jax.random.uniform(key_diag, (row_count, BLOCK_DOFS), jnp.float32, low_diag, high_diag)
    spread = jax.random.truncated_normal(key_off, -4.0, 4.0, shape, jnp.float32)
    identity = jnp.eye(BLOCK_DOFS, dtype=bool)
    scale = off_scale / jnp.sqrt(jnp.float32(BLOCK_DOFS))
    return jnp.where(identity[None], diagonal[:, :, None], spread * scale).astype(jnp.bfloat16)


def draw_fine_inverse(key, part):
    return inverse_blocks(key, ELEMENTS, 0.22, 0.44, 0.11)


def draw_coarse_inverse(key, part):
    return inverse_blocks(key, COARSE, 0.1, 0.2, 0.05)


def neighbour_lists(key, total, per_owner):
    owners = total // per_owner
    key_side, key_slot, key_edge = jax.random.split(key, 3)
    shift_by = jax.random.randint(key_side, (total, 6), -1, 2)
    slot_index = jax.random.randint(key_slot, (total, 6), 0, per_owner)
    boundary = jax.random.randint(key_edge, (total, 6), 0, 8) == 0
    owner = (jnp.arange(total, dtype=jnp.int32) // per_owner)[:, None]
    target = (owner + shift_by) % owners * per_owner + slot_index
    links = jnp.where(boundary, -1, target).astype(jnp.int32)
    return links.at[0, 0].set(total - 1).at[0, 1].set(-1)


def draw_fine_links(key, part):
    return neighbour_lists(key, ELEMENTS, E_DEV)


def draw_coarse_links(key, part):
    return neighbour_lists(key, COARSE, COLUMN)


def draw_agglomerate(key, part):
    columns = ELEMENTS // FINE_COLUMN
    scores = jax.random.randint(key, (columns, FINE_COLUMN), 0, 1048576) * FINE_COLUMN + jnp.arange(FINE_COLUMN, dtype=jnp.int32)[None, :]
    order = jnp.argsort(scores, axis=1)
    base = jnp.arange(FINE_COLUMN, dtype=jnp.int32) // AGGLOMERATE
    local_target = base[order]
    return (local_target + jnp.arange(columns, dtype=jnp.int32)[:, None] * COLUMN).reshape(-1).astype(jnp.int32)


def place_ends(result, key, smallest, largest):
    dims = result.shape
    spot = [jax.random.randint(jax.random.fold_in(key, axis), (), 0, dims[axis]) for axis in range(len(dims))]
    result = result.at[tuple(spot)].set(smallest)
    longest = dims.index(max(dims))
    spot[longest] = (spot[longest] + 1) % dims[longest]
    return result.at[tuple(spot)].set(largest)


def steps_of(stream_key, extent, shards, smallest, high):
    loudness, own = 1.0, jax.random.fold_in(stream_key, 6)
    for position, blocks in shards:
        steps = jnp.exp(jax.random.uniform(jax.random.fold_in(own, position), (blocks,), jnp.float32, smallest / len(shards), high / len(shards)))
        loudness = loudness * jnp.repeat(steps, extent[position] // blocks).reshape([-1 if axis == position else 1 for axis in range(len(extent))])
    return loudness


def centred(rng, dims, scale, bound, cuts=(), kind=jnp.bfloat16):
    drawn = scale * jax.random.normal(rng, dims, jnp.float32)
    if cuts:
        drawn = drawn * steps_of(rng, dims, cuts, -0.22, 0.18)
    return jnp.clip(drawn, -bound, bound).astype(kind)


def setup_inputs(seed: int = 0) -> dict:
    streams_of = jax.random.split(jax.random.key(seed), 10)
    right_side = centred(streams_of[0], (ELEMENTS, BLOCK_DOFS), 1.0, 6.0, ((0, 32),), jnp.float32)
    fine_inverse = draw_fine_inverse(jax.random.fold_in(streams_of[9], 71), 0)
    fine_links = draw_fine_links(jax.random.fold_in(streams_of[9], 71), 0)
    fine_faces = place_ends(jax.random.randint(streams_of[3], (ELEMENTS, 6), 0, FACE_TYPES), jax.random.fold_in(streams_of[3], 1), 0, FACE_TYPES - 1).astype(jnp.int32)
    coarse_inverse = draw_coarse_inverse(jax.random.fold_in(streams_of[9], 71), 0)
    coarse_links = draw_coarse_links(jax.random.fold_in(streams_of[9], 71), 0)
    coarse_faces = place_ends(jax.random.randint(streams_of[6], (COARSE, 6), 0, FACE_TYPES), jax.random.fold_in(streams_of[6], 1), 0, FACE_TYPES - 1).astype(jnp.int32)
    face_operators = centred(streams_of[7], (FACE_TYPES, FACE_DOFS, FACE_DOFS), (FACE_DOFS // 4) ** -0.5, 1.25)
    agglomerate = draw_agglomerate(jax.random.fold_in(streams_of[9], 71), 0)
    return dict(right_side=right_side, fine_inverse=fine_inverse, fine_links=fine_links, fine_faces=fine_faces, coarse_inverse=coarse_inverse, coarse_links=coarse_links, coarse_faces=coarse_faces, face_operators=face_operators, agglomerate=agglomerate)


OPPOSITE = (1, 0, 3, 2, 5, 4)


def take_traces(field_state):
    row_count = field_state.shape[0]
    node_cube = field_state.reshape(row_count, FIELDS, NODES, NODES, NODES)
    far_node = NODES - 1
    faces_list = (node_cube[:, :, 0], node_cube[:, :, far_node], node_cube[:, :, :, 0], node_cube[:, :, :, far_node], node_cube[:, :, :, :, 0], node_cube[:, :, :, :, far_node])
    return jnp.stack([face_slab.reshape(row_count, -1) for face_slab in faces_list], axis=1).astype(jnp.bfloat16)


def lift_faces(coupled):
    row_count = coupled.shape[0]
    pieces = coupled.reshape(row_count, 6, FIELDS, NODES, NODES)
    far_node = NODES - 1
    node_cube = jnp.zeros((row_count, FIELDS, NODES, NODES, NODES), jnp.float32)
    node_cube = node_cube.at[:, :, 0].add(pieces[:, 0])
    node_cube = node_cube.at[:, :, far_node].add(pieces[:, 1])
    node_cube = node_cube.at[:, :, :, 0].add(pieces[:, 2])
    node_cube = node_cube.at[:, :, :, far_node].add(pieces[:, 3])
    node_cube = node_cube.at[:, :, :, :, 0].add(pieces[:, 4])
    node_cube = node_cube.at[:, :, :, :, far_node].add(pieces[:, 5])
    return node_cube.reshape(row_count, -1)


def blockwise(function, arrays):
    row_count = arrays[0].shape[0]
    block_size = math.gcd(row_count, 512)
    shaped = tuple(item.reshape((row_count // block_size, block_size) + item.shape[1:]) for item in arrays)

    def apply_block(pieces):
        return function(*pieces)

    output = lax.map(apply_block, shaped)
    return output.reshape((row_count,) + output.shape[2:])


def inverse_block(inverse, vector):
    return jnp.einsum("nij,nj->ni", inverse.astype(jnp.float32), vector.astype(jnp.float32), precision=lax.Precision.HIGHEST)


def apply_inverse(inverse, vector):
    return blockwise(inverse_block, (inverse, vector))


def coupling(field_state, links, faces, face_operators):
    own_traces = take_traces(field_state)
    flat_rows = own_traces.reshape(-1, own_traces.shape[2])
    opposite = jnp.array(OPPOSITE, jnp.int32)
    row_index = jnp.maximum(links, 0) * 6 + opposite[None, :]
    face_rows = jnp.take(flat_rows, row_index.reshape(-1), axis=0).reshape(links.shape[0], 6, -1)
    face_rows = jnp.where((links >= 0)[:, :, None], face_rows, jnp.zeros_like(face_rows))

    def face_block(rows_block, kinds_block):
        chosen = jnp.take(face_operators, kinds_block.reshape(-1), axis=0).astype(jnp.float32)
        flat_block = rows_block.reshape(-1, rows_block.shape[2]).astype(jnp.float32)
        return jnp.einsum("rjk,rk->rj", chosen, flat_block, precision=lax.Precision.HIGHEST).reshape(rows_block.shape)

    coupled = blockwise(face_block, (face_rows, faces))
    return lift_faces(coupled.astype(jnp.float32))


def reference(right_side, fine_inverse, fine_links, fine_faces, coarse_inverse, coarse_links, coarse_faces, face_operators, agglomerate):
    solution = jnp.zeros(right_side.shape, jnp.float32)
    for cycle_index in range(CYCLES):
        for sweep_index in range(SWEEPS):
            if cycle_index == 0 and sweep_index == 0:
                coupled = jnp.zeros(right_side.shape, jnp.float32)
            else:
                coupled = coupling(solution, fine_links, fine_faces, face_operators)
            lowered = (right_side - coupled).astype(jnp.bfloat16)
            solution = apply_inverse(fine_inverse, lowered)
        residual = lowered.astype(jnp.float32) - coupling(solution, fine_links, fine_faces, face_operators)
        restricted = jax.ops.segment_sum(residual, agglomerate, num_segments=COARSE)
        coarse_state = apply_inverse(coarse_inverse, restricted.astype(jnp.bfloat16))
        for sweep_index in range(SWEEPS - 1):
            coupled_coarse = coupling(coarse_state, coarse_links, coarse_faces, face_operators)
            coarse_state = apply_inverse(coarse_inverse, (restricted - coupled_coarse).astype(jnp.bfloat16))
        solution = solution + jnp.take(coarse_state, agglomerate, axis=0)
    return solution
```

```python
import functools

import jax
import jax.numpy as jnp
import numpy as np
from jax import lax
from jax.experimental import pallas as pl
from jax.experimental.pallas import tpu as pltpu
from jax.sharding import PartitionSpec as P

FIELDS = 5
NODES = 4
SWEEPS = 3
CYCLES = 2
FACES = 6
FACE_DOFS = FIELDS * NODES * NODES
DOFS = FIELDS * NODES**3
SLOT = 16
LANES = 128
MESH = pl.DeviceIdType.MESH
F32 = jnp.float32
BF16 = jnp.bfloat16


def face_targets():
    cube = np.arange(DOFS).reshape(FIELDS, NODES, NODES, NODES)
    far = NODES - 1
    slabs = (
        cube[:, 0], cube[:, far], cube[:, :, 0], cube[:, :, far], cube[..., 0], cube[..., far]
    )
    return [slab.reshape(-1) for slab in slabs]


def tables():
    targets = face_targets()
    trace = np.zeros((FACES * FACE_DOFS, DOFS), np.float32)
    lift = np.zeros((DOFS, FACES * FACE_DOFS), np.float32)
    for face in range(FACES):
        rows = face * FACE_DOFS + np.arange(FACE_DOFS)
        trace[rows, targets[face ^ 1]] = 1.0
        lift[targets[face], rows] = 1.0
    return jnp.asarray(trace, BF16), jnp.asarray(lift, BF16)


def dot(a, b):
    return jnp.dot(a, b, preferred_element_type=F32)


def dot_nt(a, b):
    return lax.dot_general(a, b, (((1,), (1,)), ((), ())), preferred_element_type=F32)


def split(value):
    high = value.astype(BF16)
    return high, (value - high.astype(F32)).astype(BF16)


def flip(value):
    rows, columns = value.shape
    pad_rows, pad_columns = -rows % LANES, -columns % LANES
    if pad_columns:
        value = jnp.concatenate([value, jnp.zeros((rows, pad_columns), F32)], axis=1)
    if pad_rows:
        value = jnp.concatenate([value, jnp.zeros((pad_rows, value.shape[1]), F32)], axis=0)
    return value.T[:columns, :rows]


def kernel(
    tele,
    fine_count,
    coarse_own,
    index_ref,
    slab_ref,
    right_ref,
    inverse_hbm,
    coarse_hbm,
    operators_ref,
    trace_ref,
    lift_ref,
    out_ref,
    inverse,
    coarse_inverse,
    slabs,
    operators,
    masked,
    fine_kinds,
    coarse_kinds,
    fine_pool,
    coarse_pool,
    partials,
    right,
    state,
    lowered,
    restricted,
    coarse_state,
    load_sem,
    own_sem,
    block_send,
    block_recv,
    slab_send,
    slab_recv,
    fine_send,
    fine_recv,
    coarse_send,
    coarse_recv,
    sum_send,
    sum_recv,
):
    types = operators_ref.shape[0]
    elements = right_ref.shape[0]
    coarse = coarse_own * tele
    fine = lax.axis_index("fine")
    place = lax.axis_index("tele")
    columns = fine_count

    def around(offset):
        position = lax.rem(fine * tele + place + offset + columns * tele, columns * tele)
        return (position // tele, lax.rem(position, tele))

    def column(offset):
        return (lax.rem(fine + offset + columns, columns), place)

    def peer(offset):
        return (fine, lax.rem(place + offset, tele))

    load = pltpu.make_async_copy(inverse_hbm, inverse, load_sem)
    load.start()
    own_rows = pl.ds(place * coarse_own, coarse_own)
    own_block = pltpu.make_async_copy(coarse_hbm, coarse_inverse.at[own_rows], own_sem)
    own_block.start()

    barrier = pltpu.get_barrier_semaphore()
    partners = [around(1), around(-1), column(1), column(-1)]
    partners += [peer(j) for j in range(1, tele)]
    for partner in partners:
        pl.semaphore_signal(barrier, inc=1, device_id=partner, device_id_type=MESH)

    operators[...] = jnp.zeros_like(operators)
    for kind in range(types):
        operators[:, kind * LANES : kind * LANES + FACE_DOFS] = operators_ref[kind]
    masked[...] = jnp.zeros_like(masked)
    right[...] = flip(right_ref[...])
    lowered[...] = right[...].astype(BF16)

    def gather_matrix(rows, width):
        wanted = lax.broadcasted_iota(jnp.int32, (LANES, LANES), 0)
        return (wanted == rows).astype(F32).T[:width, : 3 * SLOT].astype(BF16)

    def kind_masks(kinds, target, width):
        for kind in range(types):
            row = (kinds == kind).astype(F32)[:, :width]
            target[kind] = jnp.broadcast_to(row, (FACE_DOFS, width)).astype(BF16)

    fine_gather = gather_matrix(index_ref[0:1, :], FACES * elements)
    kind_masks(index_ref[1:2, :], fine_kinds, FACES * elements)
    member = (
        lax.broadcasted_iota(jnp.int32, (coarse, elements), 0) == index_ref[2:3, :elements]
    ).astype(F32).astype(BF16)

    pl.semaphore_wait(barrier, len(partners))

    setup = []
    for j in range(1, tele):
        setup.append(
            pltpu.make_async_remote_copy(
                src_ref=slab_ref,
                dst_ref=slabs.at[j],
                send_sem=slab_send.at[j],
                recv_sem=slab_recv.at[j],
                device_id=peer(j),
                device_id_type=MESH,
            )
        )
        setup.append(
            pltpu.make_async_remote_copy(
                src_ref=coarse_hbm,
                dst_ref=coarse_inverse.at[own_rows],
                send_sem=block_send.at[j],
                recv_sem=block_recv.at[j],
                device_id=peer(j),
                device_id_type=MESH,
            )
        )
    for copy in setup:
        copy.start()

    def apply_inverse(blocks, vectors, width):
        lane = lax.broadcasted_iota(jnp.int32, (DOFS, width), 1)
        total = jnp.zeros((DOFS, width), F32)
        for e in range(width):
            total = jnp.where(lane == e, dot(blocks[e], vectors), total)
        return total

    def exchange(pool, send, recv, step, partner, value):
        rows = flip(value)
        if rows.shape[0] < SLOT:
            rows = jnp.concatenate(
                [rows, jnp.zeros((SLOT - rows.shape[0], DOFS), F32)], axis=0
            )
        pool[step, SLOT : 2 * SLOT, :] = rows.astype(BF16)
        copies = [
            pltpu.make_async_remote_copy(
                src_ref=pool.at[step, pl.ds(SLOT, SLOT)],
                dst_ref=pool.at[step, pl.ds(landing * SLOT, SLOT)],
                send_sem=send.at[step, side],
                recv_sem=recv.at[step, side],
                device_id=partner(offset),
                device_id_type=MESH,
            )
            for side, (offset, landing) in enumerate(((1, 0), (-1, 2)))
        ]
        for copy in copies:
            copy.start()
        for copy in copies:
            copy.wait()
        return pool[step]

    def coupling(states, gather, kinds, width):
        picked = dot(gather, states).astype(BF16)
        traces = dot_nt(trace_ref[...], picked)
        lane_face = lax.broadcasted_iota(jnp.int32, (FACE_DOFS, FACES * width), 1) // width
        rows = traces[:FACE_DOFS]
        for face in range(1, FACES):
            rows = jnp.where(
                lane_face == face, traces[face * FACE_DOFS : (face + 1) * FACE_DOFS], rows
            )
        rows = rows.astype(BF16)
        span = FACES * width
        for kind in range(types):
            masked[kind * LANES : kind * LANES + FACE_DOFS, :span] = rows * kinds[kind]
        coupled = dot(operators[...], masked[:, :span]).astype(BF16)
        stacked = jnp.concatenate(
            [coupled[:, face * width : (face + 1) * width] for face in range(FACES)], axis=0
        )
        return dot(lift_ref[...], stacked)

    load.wait()
    state[...] = apply_inverse(inverse, lowered[...], elements)

    def fine_coupling(step):
        states = exchange(fine_pool, fine_send, fine_recv, step, around, state[...])
        return coupling(states, fine_gather, fine_kinds, elements)

    for cycle in range(CYCLES):
        base = cycle * (SWEEPS + 1)

        @pl.loop(1 if cycle == 0 else 0, SWEEPS)
        def sweep(s):
            low = (right[...] - fine_coupling(base + s)).astype(BF16)
            lowered[...] = low
            state[...] = apply_inverse(inverse, low, elements)

        residual = lowered[...].astype(F32) - fine_coupling(base + SWEEPS)
        high, low = split(residual)
        partials[cycle, 0] = dot_nt(member, high) + dot_nt(member, low)
        copies = [
            pltpu.make_async_remote_copy(
                src_ref=partials.at[cycle, 0],
                dst_ref=partials.at[cycle, j],
                send_sem=sum_send.at[cycle, j],
                recv_sem=sum_recv.at[cycle, j],
                device_id=peer(j),
                device_id_type=MESH,
            )
            for j in range(1, tele)
        ]
        for copy in copies:
            copy.start()
        if cycle == 0:
            own_block.wait()
            for copy in setup:
                copy.wait()
            slab = slab_ref[...]
            for j in range(1, tele):
                slab = slab + slabs[j]
            coarse_gather = gather_matrix(slab[0:1, :] - 1, FACES * coarse)
            kind_masks(slab[1:2, :], coarse_kinds, FACES * coarse)
        for copy in copies:
            copy.wait()
        total = partials[cycle, 0]
        for j in range(1, tele):
            total = total + partials[cycle, j]
        restricted[...] = flip(total)
        coarse_state[...] = apply_inverse(
            coarse_inverse, restricted[...].astype(BF16), coarse
        )

        @pl.loop(0, SWEEPS - 1)
        def coarse_sweep(s):
            states = exchange(
                coarse_pool,
                coarse_send,
                coarse_recv,
                cycle * (SWEEPS - 1) + s,
                column,
                coarse_state[...],
            )
            low = restricted[...] - coupling(states, coarse_gather, coarse_kinds, coarse)
            coarse_state[...] = apply_inverse(coarse_inverse, low.astype(BF16), coarse)

        high, low = split(coarse_state[...])
        state[...] = state[...] + dot(high, member) + dot(low, member)

    out_ref[...] = flip(state[...])


def row_of(values, width):
    flat = values.reshape(1, -1)
    return jnp.pad(flat, ((0, 0), (0, width - flat.shape[1])))


def pool_rows(links, position, row_count, devices):
    clamped = jnp.maximum(links, 0)
    relative = (clamped // row_count - position + 1) % devices
    return jnp.where(links >= 0, relative * SLOT + clamped % row_count, -1)


def shards(
    fine_size,
    tele,
    right_side,
    fine_inverse,
    fine_links,
    fine_faces,
    coarse_inverse,
    coarse_links,
    coarse_faces,
    face_operators,
    agglomerate,
):
    elements = right_side.shape[0]
    coarse_own = coarse_inverse.shape[0]
    coarse = coarse_own * tele
    types = face_operators.shape[0]
    fine = lax.axis_index("fine")
    place = lax.axis_index("tele")
    fine_rows = pool_rows(fine_links, fine * tele + place, elements, fine_size * tele)
    index = jnp.concatenate(
        [
            jnp.pad(
                row_of(fine_rows.T, FACES * elements),
                ((0, 0), (0, LANES - FACES * elements)),
                constant_values=-1,
            ),
            row_of(fine_faces.T, LANES),
            row_of(agglomerate % coarse, LANES),
            jnp.zeros((5, LANES), jnp.int32),
        ],
        axis=0,
    )
    coarse_rows = pool_rows(coarse_links, fine, coarse, fine_size) + 1

    def spread(values):
        own = (jnp.arange(coarse, dtype=jnp.int32) // coarse_own == place)[None, :]
        return row_of(jnp.where(own, jnp.tile(values.T, (1, tele)), 0), LANES)

    slab = jnp.concatenate(
        [spread(coarse_rows), spread(coarse_faces), jnp.zeros((6, LANES), jnp.int32)], axis=0
    )
    trace, lift = tables()
    rounds = CYCLES * (SWEEPS + 1)
    coarse_rounds = CYCLES * (SWEEPS - 1)
    vmem = pl.BlockSpec(memory_space=pltpu.VMEM)
    hbm = pl.BlockSpec(memory_space=pl.ANY)
    dma = pltpu.SemaphoreType.DMA
    return pl.pallas_call(
        functools.partial(kernel, tele, fine_size, coarse_own),
        out_shape=jax.ShapeDtypeStruct(right_side.shape, F32),
        in_specs=[vmem, vmem, vmem, hbm, hbm, vmem, vmem, vmem],
        out_specs=vmem,
        scratch_shapes=[
            pltpu.VMEM(fine_inverse.shape, BF16),
            pltpu.VMEM((coarse, DOFS, DOFS), BF16),
            pltpu.VMEM((tele, 8, LANES), jnp.int32),
            pltpu.VMEM((FACE_DOFS, types * LANES), BF16),
            pltpu.VMEM((types * LANES, FACES * elements), BF16),
            pltpu.VMEM((types, FACE_DOFS, FACES * elements), BF16),
            pltpu.VMEM((types, FACE_DOFS, FACES * coarse), BF16),
            pltpu.VMEM((rounds, 3 * SLOT, DOFS), BF16),
            pltpu.VMEM((coarse_rounds, 3 * SLOT, DOFS), BF16),
            pltpu.VMEM((CYCLES, tele, coarse, DOFS), F32),
            pltpu.VMEM((DOFS, elements), F32),
            pltpu.VMEM((DOFS, elements), F32),
            pltpu.VMEM((DOFS, elements), BF16),
            pltpu.VMEM((DOFS, coarse), F32),
            pltpu.VMEM((DOFS, coarse), F32),
            dma,
            dma,
            dma((tele,)),
            dma((tele,)),
            dma((tele,)),
            dma((tele,)),
            dma((rounds, 2)),
            dma((rounds, 2)),
            dma((coarse_rounds, 2)),
            dma((coarse_rounds, 2)),
            dma((CYCLES, tele)),
            dma((CYCLES, tele)),
        ],
        compiler_params=pltpu.CompilerParams(
            collective_id=0, has_side_effects=True, vmem_limit_bytes=40 * 2**20
        ),
        name="v_cycles",
    )(index, slab, right_side, fine_inverse, coarse_inverse, face_operators, trace, lift)


def solution(mesh):
    return jax.shard_map(
        functools.partial(shards, mesh.shape["fine"], mesh.shape["tele"]),
        mesh=mesh,
        in_specs=(
            P(("fine", "tele"), None),
            P(("fine", "tele"), None, None),
            P(("fine", "tele"), None),
            P(("fine", "tele"), None),
            P(("fine", "tele"), None, None),
            P(("fine", "tele"), None),
            P(("fine", "tele"), None),
            P(),
            P(("fine", "tele")),
        ),
        out_specs=P(("fine", "tele"), None),
        check_vma=False,
    )
```

```python
import functools

import jax
import jax.numpy as jnp
import numpy as np
from jax import lax
from jax.experimental import pallas as pl
from jax.experimental.pallas import tpu as pltpu
from jax.sharding import PartitionSpec as P

FIELDS = 5
NODES = 4
SWEEPS = 3
CYCLES = 2
FACES = 6
FACE_DOFS = FIELDS * NODES * NODES
DOFS = FIELDS * NODES**3
SLOT = 16
LANES = 128
MAIN = 256
TAIL = DOFS - MAIN
VMEM_BYTES = 60 * 2**20
MESH = pl.DeviceIdType.MESH
F32 = jnp.float32
BF16 = jnp.bfloat16


def face_targets():
    cube = np.arange(DOFS).reshape(FIELDS, NODES, NODES, NODES)
    far = NODES - 1
    slabs = (
        cube[:, 0], cube[:, far], cube[:, :, 0], cube[:, :, far], cube[..., 0], cube[..., far]
    )
    return [slab.reshape(-1) for slab in slabs]


def tables():
    targets = face_targets()
    trace = np.zeros((FACES * FACE_DOFS, DOFS), np.float32)
    lift = np.zeros((DOFS, FACES * FACE_DOFS), np.float32)
    for face in range(FACES):
        rows = face * FACE_DOFS + np.arange(FACE_DOFS)
        trace[rows, targets[face ^ 1]] = 1.0
        lift[targets[face], rows] = 1.0
    return jnp.asarray(trace, BF16), jnp.asarray(lift, BF16)


def dot(a, b):
    return jnp.dot(a, b, preferred_element_type=F32)


def dot_nt(a, b):
    return lax.dot_general(a, b, (((1,), (1,)), ((), ())), preferred_element_type=F32)


def split(value):
    high = value.astype(BF16)
    return high, (value - high.astype(F32)).astype(BF16)


def flip(value):
    rows, columns = value.shape
    pad_rows, pad_columns = -rows % LANES, -columns % LANES
    if pad_columns:
        value = jnp.concatenate([value, jnp.zeros((rows, pad_columns), F32)], axis=1)
    if pad_rows:
        value = jnp.concatenate([value, jnp.zeros((pad_rows, value.shape[1]), F32)], axis=0)
    return value.T[:columns, :rows]


def kernel(
    tele,
    fine_count,
    right_hbm,
    inverse_hbm,
    links_hbm,
    faces_hbm,
    coarse_hbm,
    coarse_links_ref,
    coarse_faces_ref,
    operators_hbm,
    agglomerate_ref,
    trace_hbm,
    lift_hbm,
    out_ref,
    raw,
    coarse_raw,
    inverse,
    coarse_inverse,
    right_in,
    links,
    faces,
    operators_in,
    trace,
    lift,
    slabs,
    operators,
    masked,
    fine_kinds,
    coarse_kinds,
    fine_gather,
    coarse_gather,
    fine_pool,
    coarse_pool,
    partials,
    right,
    state,
    lowered,
    coupled,
    restricted,
    coarse_state,
    coarse_coupled,
    load_sem,
    inverse_sem,
    own_sem,
    block_send,
    block_recv,
    slab_send,
    slab_recv,
    fine_send,
    fine_recv,
    coarse_send,
    coarse_recv,
    sum_send,
    sum_recv,
):
    types = operators_in.shape[0]
    elements = right_in.shape[0]
    coarse_own = coarse_links_ref.shape[0]
    coarse = coarse_own * tele
    fine = lax.axis_index("fine")
    place = lax.axis_index("tele")
    columns = fine_count
    position = fine * tele + place

    def around(offset):
        other = lax.rem(position + offset + columns * tele, columns * tele)
        return (other // tele, lax.rem(other, tele))

    def column(offset):
        return (lax.rem(fine + offset + columns, columns), place)

    def peer(offset):
        return (fine, lax.rem(place + offset, tele))

    pairs = (
        (right_hbm, right_in),
        (links_hbm, links),
        (faces_hbm, faces),
        (operators_hbm, operators_in),
        (trace_hbm, trace),
        (lift_hbm, lift),
    )
    loads = [
        pltpu.make_async_copy(source, target, load_sem.at[i])
        for i, (source, target) in enumerate(pairs)
    ]
    own_rows = pl.ds(place * coarse_own, coarse_own)
    own_block = pltpu.make_async_copy(coarse_hbm, coarse_raw.at[own_rows], own_sem)
    blocks = [
        pltpu.make_async_copy(inverse_hbm.at[e], raw.at[e], inverse_sem.at[e])
        for e in range(elements)
    ]
    for copy in loads + blocks + [own_block]:
        copy.start()

    barrier = pltpu.get_barrier_semaphore()
    partners = [around(1), around(-1), column(1), column(-1)]
    partners += [peer(j) for j in range(1, tele)]
    for partner in partners:
        pl.semaphore_signal(barrier, inc=1, device_id=partner, device_id_type=MESH)

    def gather_matrix(wanted, centre, count, owned):
        lane = lax.broadcasted_iota(jnp.int32, (1, 3 * SLOT), 1)
        target = jnp.full((1, 3 * SLOT), -2, jnp.int32)
        for slot in range(3):
            owner = lax.rem(centre + slot - 1 + count, count)
            inside = (lane >= slot * SLOT) & (lane < slot * SLOT + owned)
            target = jnp.where(inside, owner * owned + lane - slot * SLOT, target)
        return jnp.concatenate(
            [(wanted[:, face : face + 1] == target).astype(F32) for face in range(FACES)], axis=0
        ).astype(BF16)

    def kind_masks(kinds, target, width):
        turned = flip(kinds.astype(F32))
        row = jnp.concatenate([turned[face : face + 1] for face in range(FACES)], axis=1)
        for kind in range(types):
            chosen = (row == float(kind)).astype(F32)
            target[kind] = jnp.broadcast_to(chosen, (FACE_DOFS, FACES * width)).astype(BF16)

    coupled[...] = jnp.zeros_like(coupled)
    coarse_coupled[...] = jnp.zeros_like(coarse_coupled)
    slabs[place, 0, :coarse_own, :FACES] = coarse_links_ref[...]
    slabs[place, 1, :coarse_own, :FACES] = coarse_faces_ref[...]
    lane = lax.broadcasted_iota(jnp.int32, (coarse, elements), 1)
    target = jnp.zeros((coarse, elements), jnp.int32)
    for e in range(elements):
        target = jnp.where(lane == e, agglomerate_ref[e], target)
    row = lax.broadcasted_iota(jnp.int32, (coarse, elements), 0)
    member = (target == row + fine * coarse).astype(F32).astype(BF16)

    pl.semaphore_wait(barrier, len(partners))

    setup = []
    for j in range(1, tele):
        setup.append(
            pltpu.make_async_remote_copy(
                src_ref=slabs.at[place],
                dst_ref=slabs.at[place],
                send_sem=slab_send.at[j],
                recv_sem=slab_recv.at[j],
                device_id=peer(j),
                device_id_type=MESH,
            )
        )
        setup.append(
            pltpu.make_async_remote_copy(
                src_ref=coarse_hbm,
                dst_ref=coarse_raw.at[own_rows],
                send_sem=block_send.at[j],
                recv_sem=block_recv.at[j],
                device_id=peer(j),
                device_id_type=MESH,
            )
        )
    for copy in setup:
        copy.start()

    for copy in loads:
        copy.wait()
    right[...] = flip(right_in[...])
    operators[...] = jnp.concatenate([operators_in[kind] for kind in range(types)], axis=1)
    fine_gather[...] = gather_matrix(links[...], position, columns * tele, elements)
    kind_masks(faces[...], fine_kinds, elements)

    def pack(source, target, e):
        target[:, e * MAIN : (e + 1) * MAIN] = source[e, :, :MAIN]
        if e % 2:
            at = source.shape[0] * MAIN + (e - 1) * TAIL
            target[:, at : at + 2 * TAIL] = jnp.concatenate(
                [source[e - 1, :, MAIN:], source[e, :, MAIN:]], axis=1
            )

    def apply_inverse(packed, vectors, width):
        lane = lax.broadcasted_iota(jnp.int32, (1, width), 1)
        alone = [vectors * (lane == e).astype(F32).astype(BF16) for e in range(width)]
        spread = jnp.concatenate(
            [part[:MAIN] for part in alone] + [part[MAIN:] for part in alone], axis=0
        )
        return dot(packed[...], spread)

    def exchange(pool, send, recv, step, partner, value):
        rows = flip(value)
        if rows.shape[0] < SLOT:
            rows = jnp.concatenate(
                [rows, jnp.zeros((SLOT - rows.shape[0], DOFS), F32)], axis=0
            )
        pool[step, SLOT : 2 * SLOT, :] = rows.astype(BF16)
        copies = [
            pltpu.make_async_remote_copy(
                src_ref=pool.at[step, pl.ds(SLOT, SLOT)],
                dst_ref=pool.at[step, pl.ds(landing * SLOT, SLOT)],
                send_sem=send.at[step, side],
                recv_sem=recv.at[step, side],
                device_id=partner(offset),
                device_id_type=MESH,
            )
            for side, (offset, landing) in enumerate(((1, 0), (-1, 2)))
        ]
        for copy in copies:
            copy.start()
        for copy in copies:
            copy.wait()
        return pool[step]

    def coupling(states, gather, kinds, width):
        picked = dot(gather[...], states).astype(BF16)
        traces = dot_nt(trace[...], picked)
        span = FACES * width
        lane_face = lax.broadcasted_iota(jnp.int32, (FACE_DOFS, span), 1) // width
        rows = traces[:FACE_DOFS]
        for face in range(1, FACES):
            rows = jnp.where(
                lane_face == face, traces[face * FACE_DOFS : (face + 1) * FACE_DOFS], rows
            )
        rows = rows.astype(BF16)
        for kind in range(types):
            masked[kind * FACE_DOFS : (kind + 1) * FACE_DOFS, :span] = rows * kinds[kind]
        products = dot(operators[...], masked[:, :span]).astype(BF16)
        stacked = jnp.concatenate(
            [products[:, face * width : (face + 1) * width] for face in range(FACES)], axis=0
        )
        return dot(lift[...], stacked)

    for e in range(elements):
        blocks[e].wait()
        pack(raw, inverse, e)

    @pl.loop(0, CYCLES)
    def cycle_body(cycle):
        @pl.loop(0, SWEEPS + 1)
        def sweep_body(s):
            @pl.when(cycle + s > 0)
            def couple():
                states = exchange(
                    fine_pool, fine_send, fine_recv, cycle * (SWEEPS + 1) + s, around, state[...]
                )
                coupled[...] = coupling(states, fine_gather, fine_kinds, elements)

            @pl.when(s < SWEEPS)
            def relax():
                low = (right[...] - coupled[...]).astype(BF16)
                lowered[...] = low
                state[...] = apply_inverse(inverse, low, elements)

        high, low = split(lowered[...].astype(F32) - coupled[...])
        partials[cycle, 0] = dot_nt(member, high) + dot_nt(member, low)
        copies = [
            pltpu.make_async_remote_copy(
                src_ref=partials.at[cycle, 0],
                dst_ref=partials.at[cycle, j],
                send_sem=sum_send.at[cycle, j],
                recv_sem=sum_recv.at[cycle, j],
                device_id=peer(j),
                device_id_type=MESH,
            )
            for j in range(1, tele)
        ]
        for copy in copies:
            copy.start()

        @pl.when(cycle == 0)
        def finish_setup():
            own_block.wait()
            for copy in setup:
                copy.wait()
            wanted = jnp.concatenate(
                [slabs[t, 0, :coarse_own, :FACES] for t in range(tele)], axis=0
            )
            kinds = jnp.concatenate(
                [slabs[t, 1, :coarse_own, :FACES] for t in range(tele)], axis=0
            )
            coarse_gather[...] = gather_matrix(wanted, fine, columns, coarse)
            kind_masks(kinds, coarse_kinds, coarse)
            for e in range(coarse):
                pack(coarse_raw, coarse_inverse, e)

        for copy in copies:
            copy.wait()
        total = partials[cycle, 0]
        for j in range(1, tele):
            total = total + partials[cycle, j]
        restricted[...] = flip(total)

        @pl.loop(0, SWEEPS)
        def coarse_body(s):
            @pl.when(s > 0)
            def couple():
                states = exchange(
                    coarse_pool,
                    coarse_send,
                    coarse_recv,
                    cycle * (SWEEPS - 1) + s - 1,
                    column,
                    coarse_state[...],
                )
                coarse_coupled[...] = coupling(states, coarse_gather, coarse_kinds, coarse)

            low = restricted[...]
            low = jnp.where(s > 0, low - coarse_coupled[...], low).astype(BF16)
            coarse_state[...] = apply_inverse(coarse_inverse, low, coarse)

        high, low = split(coarse_state[...])
        state[...] = state[...] + dot(high, member) + dot(low, member)

    out_ref[...] = flip(state[...])


def shards(
    fine_size,
    tele,
    right_side,
    fine_inverse,
    fine_links,
    fine_faces,
    coarse_inverse,
    coarse_links,
    coarse_faces,
    face_operators,
    agglomerate,
):
    elements = right_side.shape[0]
    coarse = coarse_inverse.shape[0] * tele
    types = face_operators.shape[0]
    trace, lift = tables()
    rounds = CYCLES * (SWEEPS + 1)
    coarse_rounds = CYCLES * (SWEEPS - 1)
    vmem = pl.BlockSpec(memory_space=pltpu.VMEM)
    smem = pl.BlockSpec(memory_space=pltpu.SMEM)
    hbm = pl.BlockSpec(memory_space=pl.ANY)
    dma = pltpu.SemaphoreType.DMA
    return pl.pallas_call(
        functools.partial(kernel, tele, fine_size),
        out_shape=jax.ShapeDtypeStruct(right_side.shape, F32),
        in_specs=[hbm, hbm, hbm, hbm, hbm, vmem, vmem, hbm, smem, hbm, hbm],
        out_specs=vmem,
        scratch_shapes=[
            pltpu.VMEM(fine_inverse.shape, BF16),
            pltpu.VMEM((coarse, DOFS, DOFS), BF16),
            pltpu.VMEM((DOFS, elements * DOFS), BF16),
            pltpu.VMEM((DOFS, coarse * DOFS), BF16),
            pltpu.VMEM(right_side.shape, F32),
            pltpu.VMEM(fine_links.shape, jnp.int32),
            pltpu.VMEM(fine_faces.shape, jnp.int32),
            pltpu.VMEM(face_operators.shape, BF16),
            pltpu.VMEM(trace.shape, BF16),
            pltpu.VMEM(lift.shape, BF16),
            pltpu.VMEM((tele, 2, 8, LANES), jnp.int32),
            pltpu.VMEM((FACE_DOFS, types * FACE_DOFS), BF16),
            pltpu.VMEM((types * FACE_DOFS, FACES * elements), BF16),
            pltpu.VMEM((types, FACE_DOFS, FACES * elements), BF16),
            pltpu.VMEM((types, FACE_DOFS, FACES * coarse), BF16),
            pltpu.VMEM((FACES * elements, 3 * SLOT), BF16),
            pltpu.VMEM((FACES * coarse, 3 * SLOT), BF16),
            pltpu.VMEM((rounds, 3 * SLOT, DOFS), BF16),
            pltpu.VMEM((coarse_rounds, 3 * SLOT, DOFS), BF16),
            pltpu.VMEM((CYCLES, tele, coarse, DOFS), F32),
            pltpu.VMEM((DOFS, elements), F32),
            pltpu.VMEM((DOFS, elements), F32),
            pltpu.VMEM((DOFS, elements), BF16),
            pltpu.VMEM((DOFS, elements), F32),
            pltpu.VMEM((DOFS, coarse), F32),
            pltpu.VMEM((DOFS, coarse), F32),
            pltpu.VMEM((DOFS, coarse), F32),
            dma((6,)),
            dma((elements,)),
            dma,
            dma((tele,)),
            dma((tele,)),
            dma((tele,)),
            dma((tele,)),
            dma((rounds, 2)),
            dma((rounds, 2)),
            dma((coarse_rounds, 2)),
            dma((coarse_rounds, 2)),
            dma((CYCLES, tele)),
            dma((CYCLES, tele)),
        ],
        compiler_params=pltpu.CompilerParams(
            collective_id=0, has_side_effects=True, vmem_limit_bytes=VMEM_BYTES
        ),
        name="v_cycles",
    )(
        right_side,
        fine_inverse,
        fine_links,
        fine_faces,
        coarse_inverse,
        coarse_links,
        coarse_faces,
        face_operators,
        agglomerate,
        trace,
        lift,
    )


def solution(mesh):
    return jax.shard_map(
        functools.partial(shards, mesh.shape["fine"], mesh.shape["tele"]),
        mesh=mesh,
        in_specs=(
            P(("fine", "tele"), None),
            P(("fine", "tele"), None, None),
            P(("fine", "tele"), None),
            P(("fine", "tele"), None),
            P(("fine", "tele"), None, None),
            P(("fine", "tele"), None),
            P(("fine", "tele"), None),
            P(),
            P(("fine", "tele")),
        ),
        out_specs=P(("fine", "tele"), None),
        check_vma=False,
    )
```

```python
import functools

import jax
import jax.numpy as jnp
import numpy as np
from jax import lax
from jax.experimental import pallas as pl
from jax.experimental.pallas import tpu as pltpu
from jax.sharding import PartitionSpec as P

FIELDS = 5
NODES = 4
SWEEPS = 3
CYCLES = 2
CHUNKS = SWEEPS + 1
FACES = 6
FACE_DOFS = FIELDS * NODES * NODES
DOFS = FIELDS * NODES**3
SLOT = 16
LANES = 128
MAIN = 256
TAIL = DOFS - MAIN
VMEM_BYTES = 60 * 2**20
MESH = pl.DeviceIdType.MESH
F32 = jnp.float32
BF16 = jnp.bfloat16


def face_targets():
    cube = np.arange(DOFS).reshape(FIELDS, NODES, NODES, NODES)
    far = NODES - 1
    slabs = (
        cube[:, 0], cube[:, far], cube[:, :, 0], cube[:, :, far], cube[..., 0], cube[..., far]
    )
    return [slab.reshape(-1) for slab in slabs]


def tables():
    targets = face_targets()
    trace = np.zeros((FACES * FACE_DOFS, DOFS), np.float32)
    lift = np.zeros((DOFS, FACES * FACE_DOFS), np.float32)
    for face in range(FACES):
        rows = face * FACE_DOFS + np.arange(FACE_DOFS)
        trace[rows, targets[face ^ 1]] = 1.0
        lift[targets[face], rows] = 1.0
    return jnp.asarray(trace, BF16), jnp.asarray(lift, BF16)


def dot(a, b):
    return jnp.dot(a, b, preferred_element_type=F32)


def dot_nt(a, b):
    return lax.dot_general(a, b, (((1,), (1,)), ((), ())), preferred_element_type=F32)


def split(value):
    high = value.astype(BF16)
    return high, (value - high.astype(F32)).astype(BF16)


def flip(value):
    rows, columns = value.shape
    pad_rows, pad_columns = -rows % LANES, -columns % LANES
    if pad_columns:
        value = jnp.concatenate([value, jnp.zeros((rows, pad_columns), F32)], axis=1)
    if pad_rows:
        value = jnp.concatenate([value, jnp.zeros((pad_rows, value.shape[1]), F32)], axis=0)
    return value.T[:columns, :rows]


def kernel(
    tele,
    fine_count,
    right_hbm,
    inverse_hbm,
    links_hbm,
    faces_hbm,
    coarse_hbm,
    coarse_links_ref,
    coarse_faces_ref,
    operators_hbm,
    agglomerate_ref,
    trace_hbm,
    lift_hbm,
    out_ref,
    raw,
    coarse_raw,
    inverse,
    coarse_inverse,
    right_in,
    links,
    faces,
    operators_in,
    trace,
    lift,
    slabs,
    operators,
    masked,
    fine_kinds,
    coarse_kinds,
    fine_gather,
    coarse_gather,
    fine_pool,
    coarse_pool,
    partials,
    right,
    state,
    lowered,
    coupled,
    restricted,
    coarse_state,
    coarse_coupled,
    load_sem,
    inverse_sem,
    own_sem,
    near_send,
    near_recv,
    block_send,
    block_recv,
    slab_send,
    slab_recv,
    fine_send,
    fine_recv,
    coarse_send,
    coarse_recv,
    sum_send,
    sum_recv,
):
    types = operators_in.shape[0]
    elements = right_in.shape[0]
    coarse_own = coarse_links_ref.shape[0]
    coarse = coarse_own * tele
    fine = lax.axis_index("fine")
    place = lax.axis_index("tele")
    columns = fine_count
    position = fine * tele + place

    def around(offset):
        other = lax.rem(position + offset + columns * tele, columns * tele)
        return (other // tele, lax.rem(other, tele))

    def column(offset):
        return (lax.rem(fine + offset + columns, columns), place)

    def peer(offset):
        return (fine, lax.rem(place + offset, tele))

    pairs = (
        (right_hbm, right_in),
        (links_hbm, links),
        (faces_hbm, faces),
        (operators_hbm, operators_in),
        (trace_hbm, trace),
        (lift_hbm, lift),
    )
    loads = [
        pltpu.make_async_copy(source, target, load_sem.at[i])
        for i, (source, target) in enumerate(pairs)
    ]
    own_block = pltpu.make_async_copy(coarse_hbm, coarse_raw, own_sem)
    blocks = [
        pltpu.make_async_copy(inverse_hbm.at[e], raw.at[e], inverse_sem.at[e])
        for e in range(elements)
    ]
    for copy in [own_block] + loads + blocks:
        copy.start()

    barrier = pltpu.get_barrier_semaphore()
    partners = [around(1), around(-1), column(1), column(-1)]
    partners += [peer(j) for j in range(1, tele)]
    for partner in partners:
        pl.semaphore_signal(barrier, inc=1, device_id=partner, device_id_type=MESH)

    def gather_matrix(wanted, centre, count, owned):
        lane = lax.broadcasted_iota(jnp.int32, (1, 3 * SLOT), 1)
        target = jnp.full((1, 3 * SLOT), -2, jnp.int32)
        for slot in range(3):
            owner = lax.rem(centre + slot - 1 + count, count)
            inside = (lane >= slot * SLOT) & (lane < slot * SLOT + owned)
            target = jnp.where(inside, owner * owned + lane - slot * SLOT, target)
        return jnp.concatenate(
            [(wanted[:, face : face + 1] == target).astype(F32) for face in range(FACES)], axis=0
        ).astype(BF16)

    def kind_masks(turned, target, width):
        row = jnp.concatenate([turned[face : face + 1] for face in range(FACES)], axis=1)
        for kind in range(types):
            chosen = (row == float(kind)).astype(F32)
            target[kind] = jnp.broadcast_to(chosen, (FACE_DOFS, FACES * width)).astype(BF16)

    coupled[...] = jnp.zeros_like(coupled)
    coarse_coupled[...] = jnp.zeros_like(coarse_coupled)
    slabs[place, 0, :coarse_own, :FACES] = coarse_links_ref[...]
    slabs[place, 1, :coarse_own, :FACES] = coarse_faces_ref[...]
    lane = lax.broadcasted_iota(jnp.int32, (coarse, elements), 1)
    target = jnp.zeros((coarse, elements), jnp.int32)
    for e in range(elements):
        target = jnp.where(lane == e, agglomerate_ref[e], target)
    row = lax.broadcasted_iota(jnp.int32, (coarse, elements), 0)
    member = (target == row + fine * coarse).astype(F32).astype(BF16)

    pl.semaphore_wait(barrier, len(partners))

    setup = [
        pltpu.make_async_remote_copy(
            src_ref=slabs.at[place],
            dst_ref=slabs.at[place],
            send_sem=slab_send.at[j],
            recv_sem=slab_recv.at[j],
            device_id=peer(j),
            device_id_type=MESH,
        )
        for j in range(1, tele)
    ]
    for copy in setup:
        copy.start()

    near = (fine, place + 1 - 2 * lax.rem(place, 2))
    far_place = lax.rem(place + 2, tele)
    far = (fine, far_place)
    chunk_rows = DOFS // CHUNKS

    def pack_own():
        own_block.wait()
        coarse_inverse[place, :, :MAIN] = coarse_raw[0, :, :MAIN]
        coarse_inverse[place, :, MAIN : 2 * MAIN] = coarse_raw[1, :, :MAIN]
        coarse_inverse[place, :, 2 * MAIN :] = jnp.concatenate(
            [coarse_raw[0, :, MAIN:], coarse_raw[1, :, MAIN:]], axis=1
        )

    def chunk_copy(owner, chunk, leg, device):
        part = coarse_inverse.at[owner, pl.ds(pl.multiple_of(chunk * chunk_rows, 16), chunk_rows)]
        return pltpu.make_async_remote_copy(
            src_ref=part,
            dst_ref=part,
            send_sem=block_send.at[leg, chunk],
            recv_sem=block_recv.at[leg, chunk],
            device_id=device,
            device_id_type=MESH,
        )

    near_copy = pltpu.make_async_remote_copy(
        src_ref=coarse_inverse.at[place],
        dst_ref=coarse_inverse.at[place],
        send_sem=near_send,
        recv_sem=near_recv,
        device_id=near,
        device_id_type=MESH,
    )
    pack_own()
    near_copy.start()

    for copy in loads:
        copy.wait()
    right[...] = flip(right_in[...])
    operators[...] = jnp.concatenate([operators_in[kind] for kind in range(types)], axis=1)
    wanted = flip(links[...].astype(F32)).astype(jnp.int32)
    fine_gather[...] = gather_matrix(wanted, position, columns * tele, elements)
    kind_masks(faces[...].astype(F32), fine_kinds, elements)

    def pack(source, target, e):
        target[:, e * MAIN : (e + 1) * MAIN] = source[e, :, :MAIN]
        if e % 2:
            at = source.shape[0] * MAIN + (e - 1) * TAIL
            target[:, at : at + 2 * TAIL] = jnp.concatenate(
                [source[e - 1, :, MAIN:], source[e, :, MAIN:]], axis=1
            )

    def apply_inverse(packed, vectors, width):
        lane = lax.broadcasted_iota(jnp.int32, (1, width), 1)
        alone = [vectors * (lane == e).astype(F32).astype(BF16) for e in range(width)]
        group = width // len(packed)
        total = None
        for i, block in enumerate(packed):
            own = alone[i * group : (i + 1) * group]
            spread = jnp.concatenate(
                [part[:MAIN] for part in own] + [part[MAIN:] for part in own], axis=0
            )
            product = dot(block, spread)
            total = product if total is None else total + product
        return total

    def exchange(pool, send, recv, step, partner, value):
        rows = flip(value)
        if rows.shape[0] < SLOT:
            rows = jnp.concatenate(
                [rows, jnp.zeros((SLOT - rows.shape[0], DOFS), F32)], axis=0
            )
        pool[step, SLOT : 2 * SLOT, :] = rows.astype(BF16)
        copies = [
            pltpu.make_async_remote_copy(
                src_ref=pool.at[step, pl.ds(SLOT, SLOT)],
                dst_ref=pool.at[step, pl.ds(landing * SLOT, SLOT)],
                send_sem=send.at[step, side],
                recv_sem=recv.at[step, side],
                device_id=partner(offset),
                device_id_type=MESH,
            )
            for side, (offset, landing) in enumerate(((1, 0), (-1, 2)))
        ]
        for copy in copies:
            copy.start()
        for copy in copies:
            copy.wait()
        return pool[step]

    def coupling(states, gather, kinds, width):
        picked = dot(gather[...], states).astype(BF16)
        traces = dot_nt(trace[...], picked)
        span = FACES * width
        lane_face = lax.broadcasted_iota(jnp.int32, (FACE_DOFS, span), 1) // width
        rows = traces[:FACE_DOFS]
        for face in range(1, FACES):
            rows = jnp.where(
                lane_face == face, traces[face * FACE_DOFS : (face + 1) * FACE_DOFS], rows
            )
        rows = rows.astype(BF16)
        for kind in range(types):
            masked[kind * FACE_DOFS : (kind + 1) * FACE_DOFS, :span] = rows * kinds[kind]
        products = dot(operators[...], masked[:, :span]).astype(BF16)
        stacked = jnp.concatenate(
            [products[:, face * width : (face + 1) * width] for face in range(FACES)], axis=0
        )
        return dot(lift[...], stacked)

    for e in range(elements):
        blocks[e].wait()
        pack(raw, inverse, e)

    chunk_copy(place, 0, 0, far).start()

    @pl.loop(0, CYCLES)
    def cycle_body(cycle):
        @pl.loop(0, SWEEPS + 1)
        def sweep_body(s):
            @pl.when(cycle + s > 0)
            def couple():
                states = exchange(
                    fine_pool, fine_send, fine_recv, cycle * (SWEEPS + 1) + s, around, state[...]
                )

                @pl.when(cycle == 0)
                def pass_on():
                    chunk_copy(place, s - 1, 0, far).wait_recv()
                    chunk_copy(far_place, s - 1, 1, near).start()
                    chunk_copy(place, s, 0, far).start()

                coupled[...] = coupling(states, fine_gather, fine_kinds, elements)

            @pl.when(s < SWEEPS)
            def relax():
                low = (right[...] - coupled[...]).astype(BF16)
                lowered[...] = low
                state[...] = apply_inverse([inverse[...]], low, elements)

        high, low = split(lowered[...].astype(F32) - coupled[...])
        partials[cycle, 0] = dot_nt(member, high) + dot_nt(member, low)
        copies = [
            pltpu.make_async_remote_copy(
                src_ref=partials.at[cycle, 0],
                dst_ref=partials.at[cycle, j],
                send_sem=sum_send.at[cycle, j],
                recv_sem=sum_recv.at[cycle, j],
                device_id=peer(j),
                device_id_type=MESH,
            )
            for j in range(1, tele)
        ]
        for copy in copies:
            copy.start()

        @pl.when(cycle == 0)
        def finish_setup():
            last = chunk_copy(place, CHUNKS - 1, 0, far)
            last.wait_recv()
            chunk_copy(far_place, CHUNKS - 1, 1, near).start()
            for copy in setup:
                copy.wait()
            wanted = jnp.concatenate(
                [slabs[t, 0, :coarse_own, :FACES] for t in range(tele)], axis=0
            )
            kinds = jnp.concatenate(
                [slabs[t, 1, :coarse_own, :FACES] for t in range(tele)], axis=0
            )
            kinds = flip(kinds.astype(F32))
            coarse_gather[...] = gather_matrix(wanted, fine, columns, coarse)
            kind_masks(kinds, coarse_kinds, coarse)
            near_copy.wait()
            for chunk in range(CHUNKS):
                chunk_copy(place, chunk, 0, far).wait_send()
                chunk_copy(far_place, chunk, 1, near).wait()

        for copy in copies:
            copy.wait()
        total = partials[cycle, 0]
        for j in range(1, tele):
            total = total + partials[cycle, j]
        restricted[...] = flip(total)

        @pl.loop(0, SWEEPS)
        def coarse_body(s):
            @pl.when(s > 0)
            def couple():
                states = exchange(
                    coarse_pool,
                    coarse_send,
                    coarse_recv,
                    cycle * (SWEEPS - 1) + s - 1,
                    column,
                    coarse_state[...],
                )
                coarse_coupled[...] = coupling(states, coarse_gather, coarse_kinds, coarse)

            low = restricted[...]
            low = jnp.where(s > 0, low - coarse_coupled[...], low).astype(BF16)
            coarse_state[...] = apply_inverse([coarse_inverse[t] for t in range(tele)], low, coarse)

        high, low = split(coarse_state[...])
        state[...] = state[...] + dot(high, member) + dot(low, member)

    out_ref[...] = flip(state[...])


def shards(
    fine_size,
    tele,
    right_side,
    fine_inverse,
    fine_links,
    fine_faces,
    coarse_inverse,
    coarse_links,
    coarse_faces,
    face_operators,
    agglomerate,
):
    elements = right_side.shape[0]
    coarse_own = coarse_inverse.shape[0]
    coarse = coarse_own * tele
    types = face_operators.shape[0]
    trace, lift = tables()
    rounds = CYCLES * (SWEEPS + 1)
    coarse_rounds = CYCLES * (SWEEPS - 1)
    vmem = pl.BlockSpec(memory_space=pltpu.VMEM)
    smem = pl.BlockSpec(memory_space=pltpu.SMEM)
    hbm = pl.BlockSpec(memory_space=pl.ANY)
    dma = pltpu.SemaphoreType.DMA
    return pl.pallas_call(
        functools.partial(kernel, tele, fine_size),
        out_shape=jax.ShapeDtypeStruct(right_side.shape, F32),
        in_specs=[hbm, hbm, hbm, hbm, hbm, vmem, vmem, hbm, smem, hbm, hbm],
        out_specs=vmem,
        scratch_shapes=[
            pltpu.VMEM(fine_inverse.shape, BF16),
            pltpu.VMEM(coarse_inverse.shape, BF16),
            pltpu.VMEM((DOFS, elements * DOFS), BF16),
            pltpu.VMEM((tele, DOFS, coarse_own * DOFS), BF16),
            pltpu.VMEM(right_side.shape, F32),
            pltpu.VMEM((FACES, elements), jnp.int32),
            pltpu.VMEM((FACES, elements), jnp.int32),
            pltpu.VMEM(face_operators.shape, BF16),
            pltpu.VMEM(trace.shape, BF16),
            pltpu.VMEM(lift.shape, BF16),
            pltpu.VMEM((tele, 2, 8, LANES), jnp.int32),
            pltpu.VMEM((FACE_DOFS, types * FACE_DOFS), BF16),
            pltpu.VMEM((types * FACE_DOFS, FACES * elements), BF16),
            pltpu.VMEM((types, FACE_DOFS, FACES * elements), BF16),
            pltpu.VMEM((types, FACE_DOFS, FACES * coarse), BF16),
            pltpu.VMEM((FACES * elements, 3 * SLOT), BF16),
            pltpu.VMEM((FACES * coarse, 3 * SLOT), BF16),
            pltpu.VMEM((rounds, 3 * SLOT, DOFS), BF16),
            pltpu.VMEM((coarse_rounds, 3 * SLOT, DOFS), BF16),
            pltpu.VMEM((CYCLES, tele, coarse, DOFS), F32),
            pltpu.VMEM((DOFS, elements), F32),
            pltpu.VMEM((DOFS, elements), F32),
            pltpu.VMEM((DOFS, elements), BF16),
            pltpu.VMEM((DOFS, elements), F32),
            pltpu.VMEM((DOFS, coarse), F32),
            pltpu.VMEM((DOFS, coarse), F32),
            pltpu.VMEM((DOFS, coarse), F32),
            dma((6,)),
            dma((elements,)),
            dma,
            dma,
            dma,
            dma((2, CHUNKS)),
            dma((2, CHUNKS)),
            dma((tele,)),
            dma((tele,)),
            dma((rounds, 2)),
            dma((rounds, 2)),
            dma((coarse_rounds, 2)),
            dma((coarse_rounds, 2)),
            dma((CYCLES, tele)),
            dma((CYCLES, tele)),
        ],
        compiler_params=pltpu.CompilerParams(
            collective_id=0, has_side_effects=True, vmem_limit_bytes=VMEM_BYTES
        ),
        name="v_cycles",
    )(
        right_side,
        fine_inverse,
        fine_links.T,
        fine_faces.T,
        coarse_inverse,
        coarse_links,
        coarse_faces,
        face_operators,
        agglomerate,
        trace,
        lift,
    )


def solution(mesh):
    return jax.shard_map(
        functools.partial(shards, mesh.shape["fine"], mesh.shape["tele"]),
        mesh=mesh,
        in_specs=(
            P(("fine", "tele"), None),
            P(("fine", "tele"), None, None),
            P(("fine", "tele"), None),
            P(("fine", "tele"), None),
            P(("fine", "tele"), None, None),
            P(("fine", "tele"), None),
            P(("fine", "tele"), None),
            P(),
            P(("fine", "tele")),
        ),
        out_specs=P(("fine", "tele"), None),
        check_vma=False,
    )
```

```python
import functools

import jax
import jax.numpy as jnp
import numpy as np
from jax import lax
from jax.experimental import pallas as pl
from jax.experimental.pallas import tpu as pltpu
from jax.sharding import PartitionSpec as P

FIELDS = 5
NODES = 4
SWEEPS = 3
CYCLES = 2
CHUNKS = SWEEPS + 1
FACES = 6
FACE_DOFS = FIELDS * NODES * NODES
DOFS = FIELDS * NODES**3
SLOT = 16
LANES = 128
MAIN = 256
TAIL = DOFS - MAIN
VMEM_BYTES = 60 * 2**20
MESH = pl.DeviceIdType.MESH
F32 = jnp.float32
BF16 = jnp.bfloat16


def face_targets():
    cube = np.arange(DOFS).reshape(FIELDS, NODES, NODES, NODES)
    far = NODES - 1
    slabs = (
        cube[:, 0], cube[:, far], cube[:, :, 0], cube[:, :, far], cube[..., 0], cube[..., far]
    )
    return [slab.reshape(-1) for slab in slabs]


def tables():
    targets = face_targets()
    trace = np.zeros((FACES * FACE_DOFS, DOFS), np.float32)
    lift = np.zeros((DOFS, FACES * FACE_DOFS), np.float32)
    for face in range(FACES):
        rows = face * FACE_DOFS + np.arange(FACE_DOFS)
        trace[rows, targets[face ^ 1]] = 1.0
        lift[targets[face], rows] = 1.0
    return jnp.asarray(trace, BF16), jnp.asarray(lift, BF16)


def dot(a, b):
    return jnp.dot(a, b, preferred_element_type=F32)


def dot_nt(a, b):
    return lax.dot_general(a, b, (((1,), (1,)), ((), ())), preferred_element_type=F32)


def split(value):
    high = value.astype(BF16)
    return high, (value - high.astype(F32)).astype(BF16)


def flip(value):
    rows, columns = value.shape
    pad_rows, pad_columns = -rows % LANES, -columns % LANES
    if pad_columns:
        value = jnp.concatenate([value, jnp.zeros((rows, pad_columns), F32)], axis=1)
    if pad_rows:
        value = jnp.concatenate([value, jnp.zeros((pad_rows, value.shape[1]), F32)], axis=0)
    return value.T[:columns, :rows]


def kernel(
    tele,
    fine_count,
    right_hbm,
    inverse_hbm,
    links_hbm,
    faces_hbm,
    coarse_hbm,
    coarse_links_hbm,
    coarse_faces_hbm,
    operators_hbm,
    agglomerate_hbm,
    trace_hbm,
    lift_hbm,
    out_ref,
    raw,
    coarse_raw,
    inverse,
    coarse_inverse,
    right_in,
    links,
    faces,
    operators_in,
    trace,
    lift,
    coarse_links,
    coarse_faces,
    targets,
    member,
    slabs,
    operators,
    masked,
    fine_kinds,
    coarse_kinds,
    fine_gather,
    coarse_gather,
    fine_pool,
    coarse_pool,
    partials,
    right,
    state,
    lowered,
    coupled,
    restricted,
    coarse_state,
    coarse_coupled,
    load_sem,
    inverse_sem,
    own_sem,
    near_send,
    near_recv,
    block_send,
    block_recv,
    slab_send,
    slab_recv,
    fine_send,
    fine_recv,
    coarse_send,
    coarse_recv,
    sum_send,
    sum_recv,
):
    types = operators_in.shape[0]
    elements = right_in.shape[0]
    coarse_own = coarse_links.shape[0]
    coarse = coarse_own * tele
    fine = lax.axis_index("fine")
    place = lax.axis_index("tele")
    columns = fine_count
    position = fine * tele + place

    def around(offset):
        other = lax.rem(position + offset + columns * tele, columns * tele)
        return (other // tele, lax.rem(other, tele))

    def column(offset):
        return (lax.rem(fine + offset + columns, columns), place)

    def peer(offset):
        return (fine, lax.rem(place + offset, tele))

    pairs = (
        (right_hbm, right_in),
        (links_hbm, links),
        (faces_hbm, faces),
        (operators_hbm, operators_in),
        (trace_hbm, trace),
        (lift_hbm, lift),
        (coarse_links_hbm, coarse_links),
        (coarse_faces_hbm, coarse_faces),
        (agglomerate_hbm, targets),
    )
    loads = [
        pltpu.make_async_copy(source, target, load_sem.at[i])
        for i, (source, target) in enumerate(pairs)
    ]
    own_block = pltpu.make_async_copy(coarse_hbm, coarse_raw, own_sem)
    blocks = [
        pltpu.make_async_copy(inverse_hbm.at[e], raw.at[e], inverse_sem.at[e])
        for e in range(elements)
    ]
    for copy in loads[:1] + blocks + [own_block] + loads[1:]:
        copy.start()

    barrier = pltpu.get_barrier_semaphore()
    partners = [around(1), around(-1), column(1), column(-1)]
    partners += [peer(j) for j in range(1, tele)]
    for partner in partners:
        pl.semaphore_signal(barrier, inc=1, device_id=partner, device_id_type=MESH)

    def gather_matrix(wanted, centre, count, owned):
        lane = lax.broadcasted_iota(jnp.int32, (1, 3 * SLOT), 1)
        target = jnp.full((1, 3 * SLOT), -2, jnp.int32)
        for slot in range(3):
            owner = lax.rem(centre + slot - 1 + count, count)
            inside = (lane >= slot * SLOT) & (lane < slot * SLOT + owned)
            target = jnp.where(inside, owner * owned + lane - slot * SLOT, target)
        return jnp.concatenate(
            [(wanted[:, face : face + 1] == target).astype(F32) for face in range(FACES)], axis=0
        ).astype(BF16)

    def kind_masks(turned, target, width):
        row = jnp.concatenate([turned[face : face + 1] for face in range(FACES)], axis=1)
        for kind in range(types):
            chosen = (row == float(kind)).astype(F32)
            target[kind] = jnp.broadcast_to(chosen, (FACE_DOFS, FACES * width)).astype(BF16)

    coupled[...] = jnp.zeros_like(coupled)
    coarse_coupled[...] = jnp.zeros_like(coarse_coupled)

    pl.semaphore_wait(barrier, len(partners))

    setup = [
        pltpu.make_async_remote_copy(
            src_ref=slabs.at[place],
            dst_ref=slabs.at[place],
            send_sem=slab_send.at[j],
            recv_sem=slab_recv.at[j],
            device_id=peer(j),
            device_id_type=MESH,
        )
        for j in range(1, tele)
    ]

    near = (fine, place + 1 - 2 * lax.rem(place, 2))
    far_place = lax.rem(place + 2, tele)
    far = (fine, far_place)
    chunk_rows = DOFS // CHUNKS

    def pack_own():
        own_block.wait()
        coarse_inverse[place, :, :MAIN] = coarse_raw[0, :, :MAIN]
        coarse_inverse[place, :, MAIN : 2 * MAIN] = coarse_raw[1, :, :MAIN]
        coarse_inverse[place, :, 2 * MAIN :] = jnp.concatenate(
            [coarse_raw[0, :, MAIN:], coarse_raw[1, :, MAIN:]], axis=1
        )

    def chunk_copy(owner, chunk, leg, device):
        part = coarse_inverse.at[owner, pl.ds(pl.multiple_of(chunk * chunk_rows, 16), chunk_rows)]
        return pltpu.make_async_remote_copy(
            src_ref=part,
            dst_ref=part,
            send_sem=block_send.at[leg, chunk],
            recv_sem=block_recv.at[leg, chunk],
            device_id=device,
            device_id_type=MESH,
        )

    near_copy = pltpu.make_async_remote_copy(
        src_ref=coarse_inverse.at[place],
        dst_ref=coarse_inverse.at[place],
        send_sem=near_send,
        recv_sem=near_recv,
        device_id=near,
        device_id_type=MESH,
    )
    def fine_tables():
        for copy in loads[1:]:
            copy.wait()
        operators[...] = jnp.concatenate([operators_in[kind] for kind in range(types)], axis=1)
        wanted = flip(links[...].astype(F32)).astype(jnp.int32)
        fine_gather[...] = gather_matrix(wanted, position, columns * tele, elements)
        kind_masks(faces[...].astype(F32), fine_kinds, elements)
        slabs[place, 0, :coarse_own, :FACES] = coarse_links[...]
        slabs[place, 1, :coarse_own, :FACES] = coarse_faces[...]
        for copy in setup:
            copy.start()
        lane = lax.broadcasted_iota(jnp.int32, (coarse, elements), 1)
        target = jnp.zeros((coarse, elements), jnp.int32)
        for e in range(elements):
            target = jnp.where(lane == e, targets[e], target)
        row = lax.broadcasted_iota(jnp.int32, (coarse, elements), 0)
        member[...] = (target == row + fine * coarse).astype(F32).astype(BF16)

    def pack(source, target, e):
        target[:, e * MAIN : (e + 1) * MAIN] = source[e, :, :MAIN]
        if e % 2:
            at = source.shape[0] * MAIN + (e - 1) * TAIL
            target[:, at : at + 2 * TAIL] = jnp.concatenate(
                [source[e - 1, :, MAIN:], source[e, :, MAIN:]], axis=1
            )

    def apply_inverse(packed, vectors, width):
        lane = lax.broadcasted_iota(jnp.int32, (1, width), 1)
        alone = [vectors * (lane == e).astype(F32).astype(BF16) for e in range(width)]
        group = width // len(packed)
        total = None
        for i, block in enumerate(packed):
            own = alone[i * group : (i + 1) * group]
            spread = jnp.concatenate(
                [part[:MAIN] for part in own] + [part[MAIN:] for part in own], axis=0
            )
            product = dot(block, spread)
            total = product if total is None else total + product
        return total

    def exchange(pool, send, recv, step, partner, value, meanwhile=lambda: None):
        rows = flip(value)
        if rows.shape[0] < SLOT:
            rows = jnp.concatenate(
                [rows, jnp.zeros((SLOT - rows.shape[0], DOFS), F32)], axis=0
            )
        pool[step, SLOT : 2 * SLOT, :] = rows.astype(BF16)
        copies = [
            pltpu.make_async_remote_copy(
                src_ref=pool.at[step, pl.ds(SLOT, SLOT)],
                dst_ref=pool.at[step, pl.ds(landing * SLOT, SLOT)],
                send_sem=send.at[step, side],
                recv_sem=recv.at[step, side],
                device_id=partner(offset),
                device_id_type=MESH,
            )
            for side, (offset, landing) in enumerate(((1, 0), (-1, 2)))
        ]
        for copy in copies:
            copy.start()
        meanwhile()
        for copy in copies:
            copy.wait()
        return pool[step]

    def coupling(states, gather, kinds, width):
        picked = dot(gather[...], states).astype(BF16)
        traces = dot_nt(trace[...], picked)
        span = FACES * width
        lane = lax.broadcasted_iota(jnp.int32, (FACE_DOFS, span), 1)
        rows = traces[:FACE_DOFS]
        for face in range(1, FACES):
            rows = jnp.where(
                lane >= face * width, traces[face * FACE_DOFS : (face + 1) * FACE_DOFS], rows
            )
        rows = rows.astype(BF16)
        for kind in range(types):
            masked[kind * FACE_DOFS : (kind + 1) * FACE_DOFS, :span] = rows * kinds[kind]
        products = dot(operators[...], masked[:, :span]).astype(BF16)
        stacked = jnp.concatenate(
            [products[:, face * width : (face + 1) * width] for face in range(FACES)], axis=0
        )
        return dot(lift[...], stacked)

    loads[0].wait()
    right[...] = flip(right_in[...])
    for e in range(elements):
        blocks[e].wait()
        pack(raw, inverse, e)

    pack_own()
    near_copy.start()
    chunk_copy(place, 0, 0, far).start()

    @pl.loop(0, CYCLES)
    def cycle_body(cycle):
        @pl.loop(0, SWEEPS + 1)
        def sweep_body(s):
            @pl.when(cycle + s > 0)
            def couple():
                def meanwhile():
                    pl.when(cycle * (SWEEPS + 1) + s == 1)(fine_tables)

                states = exchange(
                    fine_pool,
                    fine_send,
                    fine_recv,
                    cycle * (SWEEPS + 1) + s,
                    around,
                    state[...],
                    meanwhile,
                )

                @pl.when(cycle == 0)
                def pass_on():
                    chunk_copy(place, s - 1, 0, far).wait_recv()
                    chunk_copy(far_place, s - 1, 1, near).start()
                    chunk_copy(place, s, 0, far).start()

                coupled[...] = coupling(states, fine_gather, fine_kinds, elements)

            @pl.when(s < SWEEPS)
            def relax():
                low = (right[...] - coupled[...]).astype(BF16)
                lowered[...] = low
                state[...] = apply_inverse([inverse[...]], low, elements)

        high, low = split(lowered[...].astype(F32) - coupled[...])
        partials[cycle, 0] = dot_nt(member[...], high) + dot_nt(member[...], low)
        copies = [
            pltpu.make_async_remote_copy(
                src_ref=partials.at[cycle, 0],
                dst_ref=partials.at[cycle, j],
                send_sem=sum_send.at[cycle, j],
                recv_sem=sum_recv.at[cycle, j],
                device_id=peer(j),
                device_id_type=MESH,
            )
            for j in range(1, tele)
        ]
        for copy in copies:
            copy.start()

        @pl.when(cycle == 0)
        def finish_setup():
            last = chunk_copy(place, CHUNKS - 1, 0, far)
            last.wait_recv()
            chunk_copy(far_place, CHUNKS - 1, 1, near).start()
            for copy in setup:
                copy.wait()
            wanted = jnp.concatenate(
                [slabs[t, 0, :coarse_own, :FACES] for t in range(tele)], axis=0
            )
            kinds = jnp.concatenate(
                [slabs[t, 1, :coarse_own, :FACES] for t in range(tele)], axis=0
            )
            kinds = flip(kinds.astype(F32))
            coarse_gather[...] = gather_matrix(wanted, fine, columns, coarse)
            kind_masks(kinds, coarse_kinds, coarse)
            near_copy.wait()
            for chunk in range(CHUNKS):
                chunk_copy(place, chunk, 0, far).wait_send()
                chunk_copy(far_place, chunk, 1, near).wait()

        for copy in copies:
            copy.wait()
        total = partials[cycle, 0]
        for j in range(1, tele):
            total = total + partials[cycle, j]
        restricted[...] = flip(total)

        @pl.loop(0, SWEEPS)
        def coarse_body(s):
            @pl.when(s > 0)
            def couple():
                states = exchange(
                    coarse_pool,
                    coarse_send,
                    coarse_recv,
                    cycle * (SWEEPS - 1) + s - 1,
                    column,
                    coarse_state[...],
                )
                coarse_coupled[...] = coupling(states, coarse_gather, coarse_kinds, coarse)

            low = restricted[...]
            low = jnp.where(s > 0, low - coarse_coupled[...], low).astype(BF16)
            coarse_state[...] = apply_inverse([coarse_inverse[t] for t in range(tele)], low, coarse)

        high, low = split(coarse_state[...])
        state[...] = state[...] + dot(high, member[...]) + dot(low, member[...])

    out_ref[...] = flip(state[...])


def shards(
    fine_size,
    tele,
    right_side,
    fine_inverse,
    fine_links,
    fine_faces,
    coarse_inverse,
    coarse_links,
    coarse_faces,
    face_operators,
    agglomerate,
):
    elements = right_side.shape[0]
    coarse_own = coarse_inverse.shape[0]
    coarse = coarse_own * tele
    types = face_operators.shape[0]
    trace, lift = tables()
    rounds = CYCLES * (SWEEPS + 1)
    coarse_rounds = CYCLES * (SWEEPS - 1)
    vmem = pl.BlockSpec(memory_space=pltpu.VMEM)
    hbm = pl.BlockSpec(memory_space=pltpu.HBM)
    dma = pltpu.SemaphoreType.DMA
    return pl.pallas_call(
        functools.partial(kernel, tele, fine_size),
        out_shape=jax.ShapeDtypeStruct(right_side.shape, F32),
        in_specs=[hbm] * 11,
        out_specs=vmem,
        scratch_shapes=[
            pltpu.VMEM(fine_inverse.shape, BF16),
            pltpu.VMEM(coarse_inverse.shape, BF16),
            pltpu.VMEM((DOFS, elements * DOFS), BF16),
            pltpu.VMEM((tele, DOFS, coarse_own * DOFS), BF16),
            pltpu.VMEM(right_side.shape, F32),
            pltpu.VMEM((FACES, elements), jnp.int32),
            pltpu.VMEM((FACES, elements), jnp.int32),
            pltpu.VMEM(face_operators.shape, BF16),
            pltpu.VMEM(trace.shape, BF16),
            pltpu.VMEM(lift.shape, BF16),
            pltpu.VMEM(coarse_links.shape, jnp.int32),
            pltpu.VMEM(coarse_faces.shape, jnp.int32),
            pltpu.SMEM(agglomerate.shape, jnp.int32),
            pltpu.VMEM((coarse, elements), BF16),
            pltpu.VMEM((tele, 2, 8, LANES), jnp.int32),
            pltpu.VMEM((FACE_DOFS, types * FACE_DOFS), BF16),
            pltpu.VMEM((types * FACE_DOFS, FACES * elements), BF16),
            pltpu.VMEM((types, FACE_DOFS, FACES * elements), BF16),
            pltpu.VMEM((types, FACE_DOFS, FACES * coarse), BF16),
            pltpu.VMEM((FACES * elements, 3 * SLOT), BF16),
            pltpu.VMEM((FACES * coarse, 3 * SLOT), BF16),
            pltpu.VMEM((rounds, 3 * SLOT, DOFS), BF16),
            pltpu.VMEM((coarse_rounds, 3 * SLOT, DOFS), BF16),
            pltpu.VMEM((CYCLES, tele, coarse, DOFS), F32),
            pltpu.VMEM((DOFS, elements), F32),
            pltpu.VMEM((DOFS, elements), F32),
            pltpu.VMEM((DOFS, elements), BF16),
            pltpu.VMEM((DOFS, elements), F32),
            pltpu.VMEM((DOFS, coarse), F32),
            pltpu.VMEM((DOFS, coarse), F32),
            pltpu.VMEM((DOFS, coarse), F32),
            dma((9,)),
            dma((elements,)),
            dma,
            dma,
            dma,
            dma((2, CHUNKS)),
            dma((2, CHUNKS)),
            dma((tele,)),
            dma((tele,)),
            dma((rounds, 2)),
            dma((rounds, 2)),
            dma((coarse_rounds, 2)),
            dma((coarse_rounds, 2)),
            dma((CYCLES, tele)),
            dma((CYCLES, tele)),
        ],
        compiler_params=pltpu.CompilerParams(
            collective_id=0, has_side_effects=True, vmem_limit_bytes=VMEM_BYTES
        ),
        name="v_cycles",
    )(
        right_side,
        fine_inverse,
        fine_links.T,
        fine_faces.T,
        coarse_inverse,
        coarse_links,
        coarse_faces,
        face_operators,
        agglomerate,
        trace,
        lift,
    )


def solution(mesh):
    return jax.shard_map(
        functools.partial(shards, mesh.shape["fine"], mesh.shape["tele"]),
        mesh=mesh,
        in_specs=(
            P(("fine", "tele"), None),
            P(("fine", "tele"), None, None),
            P(("fine", "tele"), None),
            P(("fine", "tele"), None),
            P(("fine", "tele"), None, None),
            P(("fine", "tele"), None),
            P(("fine", "tele"), None),
            P(),
            P(("fine", "tele")),
        ),
        out_specs=P(("fine", "tele"), None),
        check_vma=False,
    )
```

```python
import functools

import jax
import jax.numpy as jnp
import numpy as np
from jax import lax
from jax.experimental import pallas as pl
from jax.experimental.pallas import tpu as pltpu
from jax.sharding import PartitionSpec as P

FIELDS = 5
NODES = 4
SWEEPS = 3
CYCLES = 2
CHUNKS = SWEEPS + 1
FACES = 6
FACE_DOFS = FIELDS * NODES * NODES
DOFS = FIELDS * NODES**3
SLOT = 16
LANES = 128
MAIN = 256
TAIL = DOFS - MAIN
VMEM_BYTES = 60 * 2**20
MESH = pl.DeviceIdType.MESH
F32 = jnp.float32
BF16 = jnp.bfloat16


def face_targets():
    cube = np.arange(DOFS).reshape(FIELDS, NODES, NODES, NODES)
    far = NODES - 1
    slabs = (
        cube[:, 0], cube[:, far], cube[:, :, 0], cube[:, :, far], cube[..., 0], cube[..., far]
    )
    return [slab.reshape(-1) for slab in slabs]


def face_nodes():
    table = np.zeros((DOFS, FACES * LANES), np.float32)
    for face, nodes in enumerate(face_targets()):
        table[nodes, face * LANES + np.arange(FACE_DOFS)] = 1.0
    return jnp.asarray(table, BF16)


def dot(a, b):
    return jnp.dot(a, b, preferred_element_type=F32)


def dot_nt(a, b):
    return lax.dot_general(a, b, (((1,), (1,)), ((), ())), preferred_element_type=F32)


def split(value):
    high = value.astype(BF16)
    return high, (value - high.astype(F32)).astype(BF16)


def flip(value):
    rows, columns = value.shape
    pad_rows, pad_columns = -rows % LANES, -columns % LANES
    if pad_columns:
        value = jnp.concatenate([value, jnp.zeros((rows, pad_columns), F32)], axis=1)
    if pad_rows:
        value = jnp.concatenate([value, jnp.zeros((pad_rows, value.shape[1]), F32)], axis=0)
    return value.T[:columns, :rows]


def kernel(
    tele,
    fine_count,
    right_hbm,
    inverse_hbm,
    links_hbm,
    faces_hbm,
    coarse_hbm,
    coarse_links_hbm,
    coarse_faces_hbm,
    operators_hbm,
    agglomerate_hbm,
    nodes_hbm,
    out_ref,
    raw,
    coarse_raw,
    inverse,
    coarse_inverse,
    right_in,
    links,
    faces,
    operators_in,
    nodes,
    coarse_links,
    coarse_faces,
    targets,
    member,
    slabs,
    operators,
    fine_kinds,
    coarse_kinds,
    fine_gather,
    coarse_gather,
    fine_pool,
    coarse_pool,
    partials,
    right,
    state,
    lowered,
    coupled,
    restricted,
    coarse_state,
    coarse_coupled,
    load_sem,
    inverse_sem,
    own_sem,
    near_send,
    near_recv,
    block_send,
    block_recv,
    slab_send,
    slab_recv,
    fine_send,
    fine_recv,
    coarse_send,
    coarse_recv,
    sum_send,
    sum_recv,
):
    types = operators_in.shape[0]
    elements = right_in.shape[0]
    coarse_own = coarse_links.shape[0]
    coarse = coarse_own * tele
    fine = lax.axis_index("fine")
    place = lax.axis_index("tele")
    columns = fine_count
    position = fine * tele + place

    def around(offset):
        other = lax.rem(position + offset + columns * tele, columns * tele)
        return (other // tele, lax.rem(other, tele))

    def column(offset):
        return (lax.rem(fine + offset + columns, columns), place)

    def peer(offset):
        return (fine, lax.rem(place + offset, tele))

    pairs = (
        (right_hbm, right_in),
        (nodes_hbm, nodes),
        (links_hbm, links),
        (faces_hbm, faces),
        (operators_hbm, operators_in),
        (coarse_links_hbm, coarse_links),
        (coarse_faces_hbm, coarse_faces),
        (agglomerate_hbm, targets),
    )
    loads = [
        pltpu.make_async_copy(source, target, load_sem.at[i])
        for i, (source, target) in enumerate(pairs)
    ]
    own_block = pltpu.make_async_copy(coarse_hbm, coarse_raw, own_sem)
    blocks = [
        pltpu.make_async_copy(inverse_hbm.at[e], raw.at[e], inverse_sem.at[e])
        for e in range(elements)
    ]
    for copy in loads[:1] + blocks + [own_block] + loads[1:]:
        copy.start()

    barrier = pltpu.get_barrier_semaphore()
    partners = [around(1), around(-1), column(1), column(-1)]
    partners += [peer(j) for j in range(1, tele)]
    for partner in partners:
        pl.semaphore_signal(barrier, inc=1, device_id=partner, device_id_type=MESH)

    def gather_matrix(wanted, centre, count, owned):
        lane = lax.broadcasted_iota(jnp.int32, (1, 3 * SLOT), 1)
        target = jnp.full((1, 3 * SLOT), -2, jnp.int32)
        for slot in range(3):
            owner = lax.rem(centre + slot - 1 + count, count)
            inside = (lane >= slot * SLOT) & (lane < slot * SLOT + owned)
            target = jnp.where(inside, owner * owned + lane - slot * SLOT, target)
        return [(wanted[:, face : face + 1] == target).astype(F32) for face in range(FACES)]

    def kind_masks(kinds, target):
        column = jnp.concatenate([kinds[:, face : face + 1] for face in range(FACES)], axis=0)
        for kind in range(types):
            chosen = (column == kind).astype(F32)
            target[kind] = jnp.broadcast_to(chosen, target.shape[1:]).astype(BF16)

    coupled[...] = jnp.zeros_like(coupled)
    coarse_coupled[...] = jnp.zeros_like(coarse_coupled)

    pl.semaphore_wait(barrier, len(partners))

    setup = [
        pltpu.make_async_remote_copy(
            src_ref=slabs.at[place],
            dst_ref=slabs.at[place],
            send_sem=slab_send.at[j],
            recv_sem=slab_recv.at[j],
            device_id=peer(j),
            device_id_type=MESH,
        )
        for j in range(1, tele)
    ]

    near = (fine, place + 1 - 2 * lax.rem(place, 2))
    far_place = lax.rem(place + 2, tele)
    far = (fine, far_place)
    chunk_rows = DOFS // CHUNKS

    def pack_own():
        own_block.wait()
        coarse_inverse[place, :, :MAIN] = coarse_raw[0, :, :MAIN]
        coarse_inverse[place, :, MAIN : 2 * MAIN] = coarse_raw[1, :, :MAIN]
        coarse_inverse[place, :, 2 * MAIN :] = jnp.concatenate(
            [coarse_raw[0, :, MAIN:], coarse_raw[1, :, MAIN:]], axis=1
        )

    def chunk_copy(owner, chunk, leg, device):
        part = coarse_inverse.at[owner, pl.ds(pl.multiple_of(chunk * chunk_rows, 16), chunk_rows)]
        return pltpu.make_async_remote_copy(
            src_ref=part,
            dst_ref=part,
            send_sem=block_send.at[leg, chunk],
            recv_sem=block_recv.at[leg, chunk],
            device_id=device,
            device_id_type=MESH,
        )

    near_copy = pltpu.make_async_remote_copy(
        src_ref=coarse_inverse.at[place],
        dst_ref=coarse_inverse.at[place],
        send_sem=near_send,
        recv_sem=near_recv,
        device_id=near,
        device_id_type=MESH,
    )
    def fine_tables():
        for copy in loads[2:]:
            copy.wait()
        operators[...] = jnp.zeros_like(operators)
        for kind in range(types):
            at = kind * LANES
            operators[at : at + FACE_DOFS, :FACE_DOFS] = flip(
                operators_in[kind].astype(F32)
            ).astype(BF16)
        wanted = flip(links[...].astype(F32)).astype(jnp.int32)
        for face, part in enumerate(gather_matrix(wanted, position, columns * tele, elements)):
            fine_gather[face] = part.astype(BF16)
        kind_masks(flip(faces[...].astype(F32)).astype(jnp.int32), fine_kinds)
        slabs[place, 0, :coarse_own, :FACES] = coarse_links[...]
        slabs[place, 1, :coarse_own, :FACES] = coarse_faces[...]
        for copy in setup:
            copy.start()
        lane = lax.broadcasted_iota(jnp.int32, (coarse, elements), 1)
        target = jnp.zeros((coarse, elements), jnp.int32)
        for e in range(elements):
            target = jnp.where(lane == e, targets[e], target)
        row = lax.broadcasted_iota(jnp.int32, (coarse, elements), 0)
        member[...] = (target == row + fine * coarse).astype(F32).astype(BF16)

    def pack(source, target, e):
        target[:, e * MAIN : (e + 1) * MAIN] = source[e, :, :MAIN]
        if e % 2:
            at = source.shape[0] * MAIN + (e - 1) * TAIL
            target[:, at : at + 2 * TAIL] = jnp.concatenate(
                [source[e - 1, :, MAIN:], source[e, :, MAIN:]], axis=1
            )

    def apply_inverse(packed, vectors, width):
        lane = lax.broadcasted_iota(jnp.int32, (1, width), 1)
        alone = [vectors * (lane == e).astype(F32).astype(BF16) for e in range(width)]
        group = width // len(packed)
        total = None
        for i, block in enumerate(packed):
            own = alone[i * group : (i + 1) * group]
            spread = jnp.concatenate(
                [part[:MAIN] for part in own] + [part[MAIN:] for part in own], axis=0
            )
            product = dot(block, spread)
            total = product if total is None else total + product
        return total

    def exchange(pool, send, recv, step, partner, value, meanwhile=lambda: None):
        rows = flip(value)
        if rows.shape[0] < SLOT:
            rows = jnp.concatenate(
                [rows, jnp.zeros((SLOT - rows.shape[0], DOFS), F32)], axis=0
            )
        pool[step, SLOT : 2 * SLOT, :] = dot(rows.astype(BF16), nodes[...]).astype(BF16)
        copies = [
            pltpu.make_async_remote_copy(
                src_ref=pool.at[step, pl.ds(SLOT, SLOT)],
                dst_ref=pool.at[step, pl.ds(landing * SLOT, SLOT)],
                send_sem=send.at[step, side],
                recv_sem=recv.at[step, side],
                device_id=partner(offset),
                device_id_type=MESH,
            )
            for side, (offset, landing) in enumerate(((1, 0), (-1, 2)))
        ]
        for copy in copies:
            copy.start()
        meanwhile()
        for copy in copies:
            copy.wait()
        return pool[step]

    def coupling(pool, gather, kinds, width):
        rows = jnp.concatenate(
            [
                dot(gather[face], pool[:, (face ^ 1) * LANES : ((face ^ 1) + 1) * LANES])
                for face in range(FACES)
            ],
            axis=0,
        ).astype(BF16)
        masked = jnp.concatenate([rows * kinds[kind] for kind in range(types)], axis=1)
        products = dot(masked, operators[...])
        stacked = jnp.concatenate(
            [products[face * width : (face + 1) * width] for face in range(FACES)], axis=1
        )
        return dot_nt(nodes[...], stacked.astype(BF16))

    loads[0].wait()
    right[...] = flip(right_in[...])
    for e in range(elements):
        blocks[e].wait()
        pack(raw, inverse, e)
    loads[1].wait()

    pack_own()
    near_copy.start()
    chunk_copy(place, 0, 0, far).start()

    @pl.loop(0, CYCLES)
    def cycle_body(cycle):
        @pl.loop(0, SWEEPS + 1)
        def sweep_body(s):
            @pl.when(cycle + s > 0)
            def couple():
                def meanwhile():
                    pl.when(cycle * (SWEEPS + 1) + s == 1)(fine_tables)

                states = exchange(
                    fine_pool,
                    fine_send,
                    fine_recv,
                    cycle * (SWEEPS + 1) + s,
                    around,
                    state[...],
                    meanwhile,
                )

                @pl.when(cycle == 0)
                def pass_on():
                    chunk_copy(place, s - 1, 0, far).wait_recv()
                    chunk_copy(far_place, s - 1, 1, near).start()
                    chunk_copy(place, s, 0, far).start()

                coupled[...] = coupling(states, fine_gather, fine_kinds, elements)

            @pl.when(s < SWEEPS)
            def relax():
                low = (right[...] - coupled[...]).astype(BF16)
                lowered[...] = low
                state[...] = apply_inverse([inverse[...]], low, elements)

        high, low = split(lowered[...].astype(F32) - coupled[...])
        partials[cycle, 0] = dot_nt(member[...], high) + dot_nt(member[...], low)
        copies = [
            pltpu.make_async_remote_copy(
                src_ref=partials.at[cycle, 0],
                dst_ref=partials.at[cycle, j],
                send_sem=sum_send.at[cycle, j],
                recv_sem=sum_recv.at[cycle, j],
                device_id=peer(j),
                device_id_type=MESH,
            )
            for j in range(1, tele)
        ]
        for copy in copies:
            copy.start()

        @pl.when(cycle == 0)
        def finish_setup():
            last = chunk_copy(place, CHUNKS - 1, 0, far)
            last.wait_recv()
            chunk_copy(far_place, CHUNKS - 1, 1, near).start()
            for copy in setup:
                copy.wait()
            wanted = jnp.concatenate(
                [slabs[t, 0, :coarse_own, :FACES] for t in range(tele)], axis=0
            )
            kinds = jnp.concatenate(
                [slabs[t, 1, :coarse_own, :FACES] for t in range(tele)], axis=0
            )
            for face, part in enumerate(gather_matrix(wanted, fine, columns, coarse)):
                coarse_gather[face] = part.astype(BF16)
            kind_masks(kinds, coarse_kinds)
            near_copy.wait()
            for chunk in range(CHUNKS):
                chunk_copy(place, chunk, 0, far).wait_send()
                chunk_copy(far_place, chunk, 1, near).wait()

        for copy in copies:
            copy.wait()
        total = partials[cycle, 0]
        for j in range(1, tele):
            total = total + partials[cycle, j]
        restricted[...] = flip(total)

        @pl.loop(0, SWEEPS)
        def coarse_body(s):
            @pl.when(s > 0)
            def couple():
                states = exchange(
                    coarse_pool,
                    coarse_send,
                    coarse_recv,
                    cycle * (SWEEPS - 1) + s - 1,
                    column,
                    coarse_state[...],
                )
                coarse_coupled[...] = coupling(states, coarse_gather, coarse_kinds, coarse)

            low = restricted[...]
            low = jnp.where(s > 0, low - coarse_coupled[...], low).astype(BF16)
            coarse_state[...] = apply_inverse([coarse_inverse[t] for t in range(tele)], low, coarse)

        high, low = split(coarse_state[...])
        state[...] = state[...] + dot(high, member[...]) + dot(low, member[...])

    out_ref[...] = flip(state[...])


def shards(
    fine_size,
    tele,
    right_side,
    fine_inverse,
    fine_links,
    fine_faces,
    coarse_inverse,
    coarse_links,
    coarse_faces,
    face_operators,
    agglomerate,
):
    elements = right_side.shape[0]
    coarse_own = coarse_inverse.shape[0]
    coarse = coarse_own * tele
    types = face_operators.shape[0]
    nodes = face_nodes()
    rounds = CYCLES * (SWEEPS + 1)
    coarse_rounds = CYCLES * (SWEEPS - 1)
    vmem = pl.BlockSpec(memory_space=pltpu.VMEM)
    hbm = pl.BlockSpec(memory_space=pltpu.HBM)
    dma = pltpu.SemaphoreType.DMA
    return pl.pallas_call(
        functools.partial(kernel, tele, fine_size),
        out_shape=jax.ShapeDtypeStruct(right_side.shape, F32),
        in_specs=[hbm] * 10,
        out_specs=vmem,
        scratch_shapes=[
            pltpu.VMEM(fine_inverse.shape, BF16),
            pltpu.VMEM(coarse_inverse.shape, BF16),
            pltpu.VMEM((DOFS, elements * DOFS), BF16),
            pltpu.VMEM((tele, DOFS, coarse_own * DOFS), BF16),
            pltpu.VMEM(right_side.shape, F32),
            pltpu.VMEM((FACES, elements), jnp.int32),
            pltpu.VMEM((FACES, elements), jnp.int32),
            pltpu.VMEM(face_operators.shape, BF16),
            pltpu.VMEM(nodes.shape, BF16),
            pltpu.VMEM(coarse_links.shape, jnp.int32),
            pltpu.VMEM(coarse_faces.shape, jnp.int32),
            pltpu.SMEM(agglomerate.shape, jnp.int32),
            pltpu.VMEM((coarse, elements), BF16),
            pltpu.VMEM((tele, 2, 8, LANES), jnp.int32),
            pltpu.VMEM((types * LANES, LANES), BF16),
            pltpu.VMEM((types, FACES * elements, LANES), BF16),
            pltpu.VMEM((types, FACES * coarse, LANES), BF16),
            pltpu.VMEM((FACES, elements, 3 * SLOT), BF16),
            pltpu.VMEM((FACES, coarse, 3 * SLOT), BF16),
            pltpu.VMEM((rounds, 3 * SLOT, FACES * LANES), BF16),
            pltpu.VMEM((coarse_rounds, 3 * SLOT, FACES * LANES), BF16),
            pltpu.VMEM((CYCLES, tele, coarse, DOFS), F32),
            pltpu.VMEM((DOFS, elements), F32),
            pltpu.VMEM((DOFS, elements), F32),
            pltpu.VMEM((DOFS, elements), BF16),
            pltpu.VMEM((DOFS, elements), F32),
            pltpu.VMEM((DOFS, coarse), F32),
            pltpu.VMEM((DOFS, coarse), F32),
            pltpu.VMEM((DOFS, coarse), F32),
            dma((8,)),
            dma((elements,)),
            dma,
            dma,
            dma,
            dma((2, CHUNKS)),
            dma((2, CHUNKS)),
            dma((tele,)),
            dma((tele,)),
            dma((rounds, 2)),
            dma((rounds, 2)),
            dma((coarse_rounds, 2)),
            dma((coarse_rounds, 2)),
            dma((CYCLES, tele)),
            dma((CYCLES, tele)),
        ],
        compiler_params=pltpu.CompilerParams(
            collective_id=0, has_side_effects=True, vmem_limit_bytes=VMEM_BYTES
        ),
        name="v_cycles",
    )(
        right_side,
        fine_inverse,
        fine_links.T,
        fine_faces.T,
        coarse_inverse,
        coarse_links,
        coarse_faces,
        face_operators,
        agglomerate,
        nodes,
    )


def solution(mesh):
    return jax.shard_map(
        functools.partial(shards, mesh.shape["fine"], mesh.shape["tele"]),
        mesh=mesh,
        in_specs=(
            P(("fine", "tele"), None),
            P(("fine", "tele"), None, None),
            P(("fine", "tele"), None),
            P(("fine", "tele"), None),
            P(("fine", "tele"), None, None),
            P(("fine", "tele"), None),
            P(("fine", "tele"), None),
            P(),
            P(("fine", "tele")),
        ),
        out_specs=P(("fine", "tele"), None),
        check_vma=False,
    )
```

```python
import functools

import jax
import jax.numpy as jnp
import numpy as np
from jax import lax
from jax.experimental import pallas as pl
from jax.experimental.pallas import tpu as pltpu
from jax.sharding import PartitionSpec as P

FIELDS = 5
NODES = 4
SWEEPS = 3
CYCLES = 2
CHUNKS = SWEEPS + 2
FACES = 6
FACE_DOFS = FIELDS * NODES * NODES
DOFS = FIELDS * NODES**3
SLOT = 16
LANES = 128
MAIN = 256
TAIL = DOFS - MAIN
VMEM_BYTES = 60 * 2**20
MESH = pl.DeviceIdType.MESH
F32 = jnp.float32
BF16 = jnp.bfloat16


def face_targets():
    cube = np.arange(DOFS).reshape(FIELDS, NODES, NODES, NODES)
    far = NODES - 1
    slabs = (
        cube[:, 0], cube[:, far], cube[:, :, 0], cube[:, :, far], cube[..., 0], cube[..., far]
    )
    return [slab.reshape(-1) for slab in slabs]


def tables():
    targets = face_targets()
    trace = np.zeros((FACES * FACE_DOFS, DOFS), np.float32)
    lift = np.zeros((DOFS, FACES * FACE_DOFS), np.float32)
    for face in range(FACES):
        rows = face * FACE_DOFS + np.arange(FACE_DOFS)
        trace[rows, targets[face ^ 1]] = 1.0
        lift[targets[face], rows] = 1.0
    return jnp.asarray(trace, BF16), jnp.asarray(lift, BF16)


def dot(a, b):
    return jnp.dot(a, b, preferred_element_type=F32)


def dot_nt(a, b):
    return lax.dot_general(a, b, (((1,), (1,)), ((), ())), preferred_element_type=F32)


def split(value):
    high = value.astype(BF16)
    return high, (value - high.astype(F32)).astype(BF16)


def flip(value):
    rows, columns = value.shape
    pad_rows, pad_columns = -rows % LANES, -columns % LANES
    if pad_columns:
        value = jnp.concatenate([value, jnp.zeros((rows, pad_columns), F32)], axis=1)
    if pad_rows:
        value = jnp.concatenate([value, jnp.zeros((pad_rows, value.shape[1]), F32)], axis=0)
    return value.T[:columns, :rows]


def kernel(
    tele,
    fine_count,
    right_hbm,
    inverse_hbm,
    links_hbm,
    faces_hbm,
    coarse_hbm,
    coarse_links_hbm,
    coarse_faces_hbm,
    operators_hbm,
    agglomerate_hbm,
    trace_hbm,
    lift_hbm,
    out_ref,
    raw,
    coarse_raw,
    inverse,
    coarse_inverse,
    right_in,
    links,
    faces,
    operators_in,
    trace,
    lift,
    coarse_links,
    coarse_faces,
    targets,
    member,
    slabs,
    operators,
    masked,
    fine_kinds,
    coarse_kinds,
    fine_gather,
    coarse_gather,
    fine_pool,
    coarse_pool,
    partials,
    right,
    state,
    lowered,
    coupled,
    restricted,
    coarse_state,
    coarse_coupled,
    load_sem,
    inverse_sem,
    own_sem,
    near_send,
    near_recv,
    block_send,
    block_recv,
    slab_send,
    slab_recv,
    fine_send,
    fine_recv,
    coarse_send,
    coarse_recv,
    sum_send,
    sum_recv,
):
    types = operators_in.shape[0]
    elements = right_in.shape[0]
    coarse_own = coarse_links.shape[0]
    coarse = coarse_own * tele
    fine = lax.axis_index("fine")
    place = lax.axis_index("tele")
    columns = fine_count
    position = fine * tele + place

    def around(offset):
        other = lax.rem(position + offset + columns * tele, columns * tele)
        return (other // tele, lax.rem(other, tele))

    def column(offset):
        return (lax.rem(fine + offset + columns, columns), place)

    def peer(offset):
        return (fine, lax.rem(place + offset, tele))

    pairs = (
        (right_hbm, right_in),
        (links_hbm, links),
        (faces_hbm, faces),
        (operators_hbm, operators_in),
        (trace_hbm, trace),
        (lift_hbm, lift),
        (coarse_links_hbm, coarse_links),
        (coarse_faces_hbm, coarse_faces),
        (agglomerate_hbm, targets),
    )
    loads = [
        pltpu.make_async_copy(source, target, load_sem.at[i])
        for i, (source, target) in enumerate(pairs)
    ]
    own_block = pltpu.make_async_copy(coarse_hbm, coarse_raw, own_sem)
    blocks = [
        pltpu.make_async_copy(inverse_hbm.at[e], raw.at[e], inverse_sem.at[e])
        for e in range(elements)
    ]
    for copy in loads[:1] + [own_block] + blocks + loads[1:]:
        copy.start()

    barrier = pltpu.get_barrier_semaphore()
    partners = [around(1), around(-1), column(1), column(-1)]
    partners += [peer(j) for j in range(1, tele)]
    for partner in partners:
        pl.semaphore_signal(barrier, inc=1, device_id=partner, device_id_type=MESH)

    def gather_matrix(wanted, centre, count, owned):
        lane = lax.broadcasted_iota(jnp.int32, (1, 3 * SLOT), 1)
        target = jnp.full((1, 3 * SLOT), -2, jnp.int32)
        for slot in range(3):
            owner = lax.rem(centre + slot - 1 + count, count)
            inside = (lane >= slot * SLOT) & (lane < slot * SLOT + owned)
            target = jnp.where(inside, owner * owned + lane - slot * SLOT, target)
        return jnp.concatenate(
            [(wanted[:, face : face + 1] == target).astype(F32) for face in range(FACES)], axis=0
        ).astype(BF16)

    def kind_masks(turned, target, width):
        row = jnp.concatenate([turned[face : face + 1] for face in range(FACES)], axis=1)
        for kind in range(types):
            chosen = (row == float(kind)).astype(F32)
            target[kind] = jnp.broadcast_to(chosen, (FACE_DOFS, FACES * width)).astype(BF16)

    coupled[...] = jnp.zeros_like(coupled)
    coarse_coupled[...] = jnp.zeros_like(coarse_coupled)

    pl.semaphore_wait(barrier, len(partners))

    setup = [
        pltpu.make_async_remote_copy(
            src_ref=slabs.at[place],
            dst_ref=slabs.at[place],
            send_sem=slab_send.at[j],
            recv_sem=slab_recv.at[j],
            device_id=peer(j),
            device_id_type=MESH,
        )
        for j in range(1, tele)
    ]

    near = (fine, place + 1 - 2 * lax.rem(place, 2))
    far_place = lax.rem(place + 2, tele)
    far = (fine, far_place)
    chunk_rows = DOFS // CHUNKS

    def pack_own():
        own_block.wait()
        coarse_inverse[place, :, :MAIN] = coarse_raw[0, :, :MAIN]
        coarse_inverse[place, :, MAIN : 2 * MAIN] = coarse_raw[1, :, :MAIN]
        coarse_inverse[place, :, 2 * MAIN :] = jnp.concatenate(
            [coarse_raw[0, :, MAIN:], coarse_raw[1, :, MAIN:]], axis=1
        )

    def chunk_copy(owner, chunk, leg, device):
        part = coarse_inverse.at[owner, pl.ds(pl.multiple_of(chunk * chunk_rows, 16), chunk_rows)]
        return pltpu.make_async_remote_copy(
            src_ref=part,
            dst_ref=part,
            send_sem=block_send.at[leg, chunk],
            recv_sem=block_recv.at[leg, chunk],
            device_id=device,
            device_id_type=MESH,
        )

    near_copy = pltpu.make_async_remote_copy(
        src_ref=coarse_inverse.at[place],
        dst_ref=coarse_inverse.at[place],
        send_sem=near_send,
        recv_sem=near_recv,
        device_id=near,
        device_id_type=MESH,
    )
    def fine_tables():
        for copy in loads[1:]:
            copy.wait()
        operators[...] = jnp.concatenate([operators_in[kind] for kind in range(types)], axis=1)
        wanted = flip(links[...].astype(F32)).astype(jnp.int32)
        fine_gather[...] = gather_matrix(wanted, position, columns * tele, elements)
        kind_masks(faces[...].astype(F32), fine_kinds, elements)
        slabs[place, 0, :coarse_own, :FACES] = coarse_links[...]
        slabs[place, 1, :coarse_own, :FACES] = coarse_faces[...]
        for copy in setup:
            copy.start()
        lane = lax.broadcasted_iota(jnp.int32, (coarse, elements), 1)
        target = jnp.zeros((coarse, elements), jnp.int32)
        for e in range(elements):
            target = jnp.where(lane == e, targets[e], target)
        row = lax.broadcasted_iota(jnp.int32, (coarse, elements), 0)
        member[...] = (target == row + fine * coarse).astype(F32).astype(BF16)

    def pack(source, target, e):
        target[:, e * MAIN : (e + 1) * MAIN] = source[e, :, :MAIN]
        if e % 2:
            at = source.shape[0] * MAIN + (e - 1) * TAIL
            target[:, at : at + 2 * TAIL] = jnp.concatenate(
                [source[e - 1, :, MAIN:], source[e, :, MAIN:]], axis=1
            )

    def apply_inverse(packed, vectors, width):
        lane = lax.broadcasted_iota(jnp.int32, (1, width), 1)
        alone = [vectors * (lane == e).astype(F32).astype(BF16) for e in range(width)]
        group = width // len(packed)
        total = None
        for i, block in enumerate(packed):
            own = alone[i * group : (i + 1) * group]
            spread = jnp.concatenate(
                [part[:MAIN] for part in own] + [part[MAIN:] for part in own], axis=0
            )
            product = dot(block, spread)
            total = product if total is None else total + product
        return total

    def exchange(pool, send, recv, step, partner, value, meanwhile=lambda: None):
        rows = flip(value)
        if rows.shape[0] < SLOT:
            rows = jnp.concatenate(
                [rows, jnp.zeros((SLOT - rows.shape[0], DOFS), F32)], axis=0
            )
        pool[step, SLOT : 2 * SLOT, :] = rows.astype(BF16)
        copies = [
            pltpu.make_async_remote_copy(
                src_ref=pool.at[step, pl.ds(SLOT, SLOT)],
                dst_ref=pool.at[step, pl.ds(landing * SLOT, SLOT)],
                send_sem=send.at[step, side],
                recv_sem=recv.at[step, side],
                device_id=partner(offset),
                device_id_type=MESH,
            )
            for side, (offset, landing) in enumerate(((1, 0), (-1, 2)))
        ]
        for copy in copies:
            copy.start()
        meanwhile()
        for copy in copies:
            copy.wait()
        return pool[step]

    def coupling(states, gather, kinds, width):
        picked = dot(gather[...], states).astype(BF16)
        traces = dot_nt(trace[...], picked)
        span = FACES * width
        lane = lax.broadcasted_iota(jnp.int32, (FACE_DOFS, span), 1)
        rows = traces[:FACE_DOFS]
        for face in range(1, FACES):
            rows = jnp.where(
                lane >= face * width, traces[face * FACE_DOFS : (face + 1) * FACE_DOFS], rows
            )
        rows = rows.astype(BF16)
        for kind in range(types):
            masked[kind * FACE_DOFS : (kind + 1) * FACE_DOFS, :span] = rows * kinds[kind]
        products = dot(operators[...], masked[:, :span]).astype(BF16)
        stacked = jnp.concatenate(
            [products[:, face * width : (face + 1) * width] for face in range(FACES)], axis=0
        )
        return dot(lift[...], stacked)

    pack_own()
    chunk_copy(place, 0, 0, far).start()
    chunk_copy(place, 1, 0, far).start()
    near_copy.start()

    loads[0].wait()
    right[...] = flip(right_in[...])
    for e in range(elements):
        blocks[e].wait()
        pack(raw, inverse, e)

    @pl.loop(0, CYCLES)
    def cycle_body(cycle):
        @pl.loop(0, SWEEPS + 1)
        def sweep_body(s):
            @pl.when(cycle + s > 0)
            def couple():
                def meanwhile():
                    pl.when(cycle * (SWEEPS + 1) + s == 1)(fine_tables)

                states = exchange(
                    fine_pool,
                    fine_send,
                    fine_recv,
                    cycle * (SWEEPS + 1) + s,
                    around,
                    state[...],
                    meanwhile,
                )

                @pl.when(cycle == 0)
                def pass_on():
                    @pl.when(s == 1)
                    def first():
                        chunk_copy(place, 0, 0, far).wait_recv()
                        chunk_copy(far_place, 0, 1, near).start()

                    chunk_copy(place, s, 0, far).wait_recv()
                    chunk_copy(far_place, s, 1, near).start()
                    chunk_copy(place, s + 1, 0, far).start()

                coupled[...] = coupling(states, fine_gather, fine_kinds, elements)

            @pl.when(s < SWEEPS)
            def relax():
                low = (right[...] - coupled[...]).astype(BF16)
                lowered[...] = low
                state[...] = apply_inverse([inverse[...]], low, elements)

        high, low = split(lowered[...].astype(F32) - coupled[...])
        partials[cycle, 0] = dot_nt(member[...], high) + dot_nt(member[...], low)
        copies = [
            pltpu.make_async_remote_copy(
                src_ref=partials.at[cycle, 0],
                dst_ref=partials.at[cycle, j],
                send_sem=sum_send.at[cycle, j],
                recv_sem=sum_recv.at[cycle, j],
                device_id=peer(j),
                device_id_type=MESH,
            )
            for j in range(1, tele)
        ]
        for copy in copies:
            copy.start()

        @pl.when(cycle == 0)
        def finish_setup():
            last = chunk_copy(place, CHUNKS - 1, 0, far)
            last.wait_recv()
            chunk_copy(far_place, CHUNKS - 1, 1, near).start()
            for copy in setup:
                copy.wait()
            wanted = jnp.concatenate(
                [slabs[t, 0, :coarse_own, :FACES] for t in range(tele)], axis=0
            )
            kinds = jnp.concatenate(
                [slabs[t, 1, :coarse_own, :FACES] for t in range(tele)], axis=0
            )
            kinds = flip(kinds.astype(F32))
            coarse_gather[...] = gather_matrix(wanted, fine, columns, coarse)
            kind_masks(kinds, coarse_kinds, coarse)
            near_copy.wait()
            for chunk in range(CHUNKS):
                chunk_copy(place, chunk, 0, far).wait_send()
                chunk_copy(far_place, chunk, 1, near).wait()

        for copy in copies:
            copy.wait()
        total = partials[cycle, 0]
        for j in range(1, tele):
            total = total + partials[cycle, j]
        restricted[...] = flip(total)

        @pl.loop(0, SWEEPS)
        def coarse_body(s):
            @pl.when(s > 0)
            def couple():
                states = exchange(
                    coarse_pool,
                    coarse_send,
                    coarse_recv,
                    cycle * (SWEEPS - 1) + s - 1,
                    column,
                    coarse_state[...],
                )
                coarse_coupled[...] = coupling(states, coarse_gather, coarse_kinds, coarse)

            low = restricted[...]
            low = jnp.where(s > 0, low - coarse_coupled[...], low).astype(BF16)
            coarse_state[...] = apply_inverse([coarse_inverse[t] for t in range(tele)], low, coarse)

        high, low = split(coarse_state[...])
        state[...] = state[...] + dot(high, member[...]) + dot(low, member[...])

    out_ref[...] = flip(state[...])


def shards(
    fine_size,
    tele,
    right_side,
    fine_inverse,
    fine_links,
    fine_faces,
    coarse_inverse,
    coarse_links,
    coarse_faces,
    face_operators,
    agglomerate,
):
    elements = right_side.shape[0]
    coarse_own = coarse_inverse.shape[0]
    coarse = coarse_own * tele
    types = face_operators.shape[0]
    trace, lift = tables()
    rounds = CYCLES * (SWEEPS + 1)
    coarse_rounds = CYCLES * (SWEEPS - 1)
    vmem = pl.BlockSpec(memory_space=pltpu.VMEM)
    hbm = pl.BlockSpec(memory_space=pltpu.HBM)
    dma = pltpu.SemaphoreType.DMA
    return pl.pallas_call(
        functools.partial(kernel, tele, fine_size),
        out_shape=jax.ShapeDtypeStruct(right_side.shape, F32),
        in_specs=[hbm] * 11,
        out_specs=vmem,
        scratch_shapes=[
            pltpu.VMEM(fine_inverse.shape, BF16),
            pltpu.VMEM(coarse_inverse.shape, BF16),
            pltpu.VMEM((DOFS, elements * DOFS), BF16),
            pltpu.VMEM((tele, DOFS, coarse_own * DOFS), BF16),
            pltpu.VMEM(right_side.shape, F32),
            pltpu.VMEM((FACES, elements), jnp.int32),
            pltpu.VMEM((FACES, elements), jnp.int32),
            pltpu.VMEM(face_operators.shape, BF16),
            pltpu.VMEM(trace.shape, BF16),
            pltpu.VMEM(lift.shape, BF16),
            pltpu.VMEM(coarse_links.shape, jnp.int32),
            pltpu.VMEM(coarse_faces.shape, jnp.int32),
            pltpu.SMEM(agglomerate.shape, jnp.int32),
            pltpu.VMEM((coarse, elements), BF16),
            pltpu.VMEM((tele, 2, 8, LANES), jnp.int32),
            pltpu.VMEM((FACE_DOFS, types * FACE_DOFS), BF16),
            pltpu.VMEM((types * FACE_DOFS, FACES * elements), BF16),
            pltpu.VMEM((types, FACE_DOFS, FACES * elements), BF16),
            pltpu.VMEM((types, FACE_DOFS, FACES * coarse), BF16),
            pltpu.VMEM((FACES * elements, 3 * SLOT), BF16),
            pltpu.VMEM((FACES * coarse, 3 * SLOT), BF16),
            pltpu.VMEM((rounds, 3 * SLOT, DOFS), BF16),
            pltpu.VMEM((coarse_rounds, 3 * SLOT, DOFS), BF16),
            pltpu.VMEM((CYCLES, tele, coarse, DOFS), F32),
            pltpu.VMEM((DOFS, elements), F32),
            pltpu.VMEM((DOFS, elements), F32),
            pltpu.VMEM((DOFS, elements), BF16),
            pltpu.VMEM((DOFS, elements), F32),
            pltpu.VMEM((DOFS, coarse), F32),
            pltpu.VMEM((DOFS, coarse), F32),
            pltpu.VMEM((DOFS, coarse), F32),
            dma((9,)),
            dma((elements,)),
            dma,
            dma,
            dma,
            dma((2, CHUNKS)),
            dma((2, CHUNKS)),
            dma((tele,)),
            dma((tele,)),
            dma((rounds, 2)),
            dma((rounds, 2)),
            dma((coarse_rounds, 2)),
            dma((coarse_rounds, 2)),
            dma((CYCLES, tele)),
            dma((CYCLES, tele)),
        ],
        compiler_params=pltpu.CompilerParams(
            collective_id=0, has_side_effects=True, vmem_limit_bytes=VMEM_BYTES
        ),
        name="v_cycles",
    )(
        right_side,
        fine_inverse,
        fine_links.T,
        fine_faces.T,
        coarse_inverse,
        coarse_links,
        coarse_faces,
        face_operators,
        agglomerate,
        trace,
        lift,
    )


def solution(mesh):
    return jax.shard_map(
        functools.partial(shards, mesh.shape["fine"], mesh.shape["tele"]),
        mesh=mesh,
        in_specs=(
            P(("fine", "tele"), None),
            P(("fine", "tele"), None, None),
            P(("fine", "tele"), None),
            P(("fine", "tele"), None),
            P(("fine", "tele"), None, None),
            P(("fine", "tele"), None),
            P(("fine", "tele"), None),
            P(),
            P(("fine", "tele")),
        ),
        out_specs=P(("fine", "tele"), None),
        check_vma=False,
    )
```

```python
import functools

import jax
import jax.numpy as jnp
import numpy as np
from jax import lax
from jax.experimental import pallas as pl
from jax.experimental.pallas import tpu as pltpu
from jax.sharding import PartitionSpec as P

FIELDS = 5
NODES = 4
SWEEPS = 3
CYCLES = 2
CHUNKS = SWEEPS + 1
FACES = 6
FACE_DOFS = FIELDS * NODES * NODES
DOFS = FIELDS * NODES**3
SLOT = 16
LANES = 128
MAIN = 256
TAIL = DOFS - MAIN
VMEM_BYTES = 60 * 2**20
MESH = pl.DeviceIdType.MESH
F32 = jnp.float32
BF16 = jnp.bfloat16


def face_targets():
    cube = np.arange(DOFS).reshape(FIELDS, NODES, NODES, NODES)
    far = NODES - 1
    slabs = (
        cube[:, 0], cube[:, far], cube[:, :, 0], cube[:, :, far], cube[..., 0], cube[..., far]
    )
    return [slab.reshape(-1) for slab in slabs]


def tables():
    targets = face_targets()
    trace = np.zeros((FACES * FACE_DOFS, DOFS), np.float32)
    lift = np.zeros((DOFS, FACES * FACE_DOFS), np.float32)
    for face in range(FACES):
        rows = face * FACE_DOFS + np.arange(FACE_DOFS)
        trace[rows, targets[face ^ 1]] = 1.0
        lift[targets[face], rows] = 1.0
    return jnp.asarray(trace, BF16), jnp.asarray(lift, BF16)


def dot(a, b):
    return jnp.dot(a, b, preferred_element_type=F32)


def dot_nt(a, b):
    return lax.dot_general(a, b, (((1,), (1,)), ((), ())), preferred_element_type=F32)


def split(value):
    high = value.astype(BF16)
    return high, (value - high.astype(F32)).astype(BF16)


def flip(value):
    rows, columns = value.shape
    pad_rows, pad_columns = -rows % LANES, -columns % LANES
    if pad_columns:
        value = jnp.concatenate([value, jnp.zeros((rows, pad_columns), F32)], axis=1)
    if pad_rows:
        value = jnp.concatenate([value, jnp.zeros((pad_rows, value.shape[1]), F32)], axis=0)
    return value.T[:columns, :rows]


def kernel(
    tele,
    fine_count,
    right_hbm,
    inverse_hbm,
    links_hbm,
    faces_hbm,
    coarse_hbm,
    coarse_links_hbm,
    coarse_faces_hbm,
    operators_hbm,
    agglomerate_hbm,
    trace_hbm,
    lift_hbm,
    out_ref,
    raw,
    coarse_raw,
    inverse,
    coarse_inverse,
    right_in,
    links,
    faces,
    operators_in,
    trace,
    lift,
    coarse_links,
    coarse_faces,
    targets,
    member,
    slabs,
    operators,
    masked,
    fine_kinds,
    coarse_kinds,
    fine_gather,
    coarse_gather,
    fine_pool,
    coarse_pool,
    partials,
    right,
    state,
    lowered,
    coupled,
    restricted,
    coarse_state,
    coarse_coupled,
    load_sem,
    inverse_sem,
    own_sem,
    near_send,
    near_recv,
    block_send,
    block_recv,
    slab_send,
    slab_recv,
    fine_send,
    fine_recv,
    coarse_send,
    coarse_recv,
    sum_send,
    sum_recv,
):
    types = operators_in.shape[0]
    elements = right_in.shape[0]
    coarse_own = coarse_links.shape[0]
    coarse = coarse_own * tele
    fine = lax.axis_index("fine")
    place = lax.axis_index("tele")
    columns = fine_count
    position = fine * tele + place

    def around(offset):
        other = lax.rem(position + offset + columns * tele, columns * tele)
        return (other // tele, lax.rem(other, tele))

    def column(offset):
        return (lax.rem(fine + offset + columns, columns), place)

    def peer(offset):
        return (fine, lax.rem(place + offset, tele))

    pairs = (
        (right_hbm, right_in),
        (links_hbm, links),
        (faces_hbm, faces),
        (operators_hbm, operators_in),
        (trace_hbm, trace),
        (lift_hbm, lift),
        (coarse_links_hbm, coarse_links),
        (coarse_faces_hbm, coarse_faces),
        (agglomerate_hbm, targets),
    )
    loads = [
        pltpu.make_async_copy(source, target, load_sem.at[i])
        for i, (source, target) in enumerate(pairs)
    ]
    own_block = pltpu.make_async_copy(coarse_hbm, coarse_raw, own_sem)
    blocks = [
        pltpu.make_async_copy(inverse_hbm.at[e], raw.at[e], inverse_sem.at[e])
        for e in range(elements)
    ]
    for copy in loads[:1] + blocks + [own_block] + loads[1:]:
        copy.start()

    barrier = pltpu.get_barrier_semaphore()
    partners = [around(1), around(-1), column(1), column(-1)]
    partners += [peer(j) for j in range(1, tele)]
    for partner in partners:
        pl.semaphore_signal(barrier, inc=1, device_id=partner, device_id_type=MESH)

    def gather_matrix(wanted, centre, count, owned):
        lane = lax.broadcasted_iota(jnp.int32, (1, 3 * SLOT), 1)
        target = jnp.full((1, 3 * SLOT), -2, jnp.int32)
        for slot in range(3):
            owner = lax.rem(centre + slot - 1 + count, count)
            inside = (lane >= slot * SLOT) & (lane < slot * SLOT + owned)
            target = jnp.where(inside, owner * owned + lane - slot * SLOT, target)
        return jnp.concatenate(
            [(wanted[:, face : face + 1] == target).astype(F32) for face in range(FACES)], axis=0
        ).astype(BF16)

    def kind_masks(turned, target, width):
        row = jnp.concatenate([turned[face : face + 1] for face in range(FACES)], axis=1)
        for kind in range(types):
            chosen = (row == float(kind)).astype(F32)
            target[kind] = jnp.broadcast_to(chosen, (FACE_DOFS, FACES * width)).astype(BF16)

    coupled[...] = jnp.zeros_like(coupled)
    coarse_coupled[...] = jnp.zeros_like(coarse_coupled)

    pl.semaphore_wait(barrier, len(partners))

    setup = [
        pltpu.make_async_remote_copy(
            src_ref=slabs.at[place],
            dst_ref=slabs.at[place],
            send_sem=slab_send.at[j],
            recv_sem=slab_recv.at[j],
            device_id=peer(j),
            device_id_type=MESH,
        )
        for j in range(1, tele)
    ]

    near = (fine, place + 1 - 2 * lax.rem(place, 2))
    far_place = lax.rem(place + 2, tele)
    far = (fine, far_place)
    chunk_rows = DOFS // CHUNKS

    def pack_own():
        own_block.wait()
        coarse_inverse[place, :, :MAIN] = coarse_raw[0, :, :MAIN]
        coarse_inverse[place, :, MAIN : 2 * MAIN] = coarse_raw[1, :, :MAIN]
        coarse_inverse[place, :, 2 * MAIN :] = jnp.concatenate(
            [coarse_raw[0, :, MAIN:], coarse_raw[1, :, MAIN:]], axis=1
        )

    def chunk_copy(owner, chunk, leg, device):
        part = coarse_inverse.at[owner, pl.ds(pl.multiple_of(chunk * chunk_rows, 16), chunk_rows)]
        return pltpu.make_async_remote_copy(
            src_ref=part,
            dst_ref=part,
            send_sem=block_send.at[leg, chunk],
            recv_sem=block_recv.at[leg, chunk],
            device_id=device,
            device_id_type=MESH,
        )

    near_copy = pltpu.make_async_remote_copy(
        src_ref=coarse_inverse.at[place],
        dst_ref=coarse_inverse.at[place],
        send_sem=near_send,
        recv_sem=near_recv,
        device_id=near,
        device_id_type=MESH,
    )
    def fine_tables():
        for copy in loads[1:]:
            copy.wait()
        operators[...] = jnp.concatenate([operators_in[kind] for kind in range(types)], axis=1)
        wanted = flip(links[...].astype(F32)).astype(jnp.int32)
        fine_gather[...] = gather_matrix(wanted, position, columns * tele, elements)
        kind_masks(faces[...].astype(F32), fine_kinds, elements)
        slabs[place, 0, :coarse_own, :FACES] = coarse_links[...]
        slabs[place, 1, :coarse_own, :FACES] = coarse_faces[...]
        for copy in setup:
            copy.start()
        lane = lax.broadcasted_iota(jnp.int32, (coarse, elements), 1)
        target = jnp.zeros((coarse, elements), jnp.int32)
        for e in range(elements):
            target = jnp.where(lane == e, targets[e], target)
        row = lax.broadcasted_iota(jnp.int32, (coarse, elements), 0)
        member[...] = (target == row + fine * coarse).astype(F32).astype(BF16)

    def pack(source, target, e):
        target[:, e * MAIN : (e + 1) * MAIN] = source[e, :, :MAIN]
        if e % 2:
            at = source.shape[0] * MAIN + (e - 1) * TAIL
            target[:, at : at + 2 * TAIL] = jnp.concatenate(
                [source[e - 1, :, MAIN:], source[e, :, MAIN:]], axis=1
            )

    def apply_inverse(packed, vectors, width):
        lane = lax.broadcasted_iota(jnp.int32, (1, width), 1)
        alone = [vectors * (lane == e).astype(F32).astype(BF16) for e in range(width)]
        spread = [part[:MAIN] for part in alone] + [part[MAIN:] for part in alone]
        if len(packed.shape) == 2:
            depth = width * DOFS // 5
            count = width // 4
            pieces = [spread[i * count : (i + 1) * count] for i in range(4)] + [spread[width:]]
            products = [
                dot(packed[:, i * depth : (i + 1) * depth], jnp.concatenate(piece, axis=0))
                for i, piece in enumerate(pieces)
            ]
        else:
            group = width // packed.shape[0]
            products = [
                dot(
                    packed[i],
                    jnp.concatenate(
                        spread[i * group : (i + 1) * group]
                        + spread[width + i * group : width + (i + 1) * group],
                        axis=0,
                    ),
                )
                for i in range(packed.shape[0])
            ]
        while len(products) > 1:
            products = [sum(products[i : i + 2]) for i in range(0, len(products), 2)]
        return products[0]

    def exchange(pool, send, recv, step, partner, value, meanwhile=lambda: None):
        rows = flip(value)
        if rows.shape[0] < SLOT:
            rows = jnp.concatenate(
                [rows, jnp.zeros((SLOT - rows.shape[0], DOFS), F32)], axis=0
            )
        pool[step, SLOT : 2 * SLOT, :] = rows.astype(BF16)
        copies = [
            pltpu.make_async_remote_copy(
                src_ref=pool.at[step, pl.ds(SLOT, SLOT)],
                dst_ref=pool.at[step, pl.ds(landing * SLOT, SLOT)],
                send_sem=send.at[step, side],
                recv_sem=recv.at[step, side],
                device_id=partner(offset),
                device_id_type=MESH,
            )
            for side, (offset, landing) in enumerate(((1, 0), (-1, 2)))
        ]
        for copy in copies:
            copy.start()
        meanwhile()
        for copy in copies:
            copy.wait()
        return pool[step]

    def coupling(states, gather, kinds, width):
        picked = dot(gather[...], states).astype(BF16)
        traces = dot_nt(trace[...], picked)
        span = FACES * width
        lane = lax.broadcasted_iota(jnp.int32, (FACE_DOFS, span), 1)
        rows = traces[:FACE_DOFS]
        for face in range(1, FACES):
            rows = jnp.where(
                lane >= face * width, traces[face * FACE_DOFS : (face + 1) * FACE_DOFS], rows
            )
        rows = rows.astype(BF16)
        for kind in range(types):
            masked[kind * FACE_DOFS : (kind + 1) * FACE_DOFS, :span] = rows * kinds[kind]
        products = dot(operators[...], masked[:, :span]).astype(BF16)
        stacked = jnp.concatenate(
            [products[:, face * width : (face + 1) * width] for face in range(FACES)], axis=0
        )
        return dot(lift[...], stacked)

    loads[0].wait()
    right[...] = flip(right_in[...])
    for e in range(elements):
        blocks[e].wait()
        pack(raw, inverse, e)

    pack_own()
    near_copy.start()
    chunk_copy(place, 0, 0, far).start()

    @pl.loop(0, CYCLES)
    def cycle_body(cycle):
        @pl.loop(0, SWEEPS + 1)
        def sweep_body(s):
            @pl.when(cycle + s > 0)
            def couple():
                def meanwhile():
                    pl.when(cycle * (SWEEPS + 1) + s == 1)(fine_tables)

                states = exchange(
                    fine_pool,
                    fine_send,
                    fine_recv,
                    cycle * (SWEEPS + 1) + s,
                    around,
                    state[...],
                    meanwhile,
                )

                @pl.when(cycle == 0)
                def pass_on():
                    chunk_copy(place, s - 1, 0, far).wait_recv()
                    chunk_copy(far_place, s - 1, 1, near).start()
                    chunk_copy(place, s, 0, far).start()

                coupled[...] = coupling(states, fine_gather, fine_kinds, elements)

            @pl.when(s < SWEEPS)
            def relax():
                low = (right[...] - coupled[...]).astype(BF16)
                lowered[...] = low
                state[...] = apply_inverse(inverse, low, elements)

        high, low = split(lowered[...].astype(F32) - coupled[...])
        partials[cycle, 0] = dot_nt(member[...], high) + dot_nt(member[...], low)
        copies = [
            pltpu.make_async_remote_copy(
                src_ref=partials.at[cycle, 0],
                dst_ref=partials.at[cycle, j],
                send_sem=sum_send.at[cycle, j],
                recv_sem=sum_recv.at[cycle, j],
                device_id=peer(j),
                device_id_type=MESH,
            )
            for j in range(1, tele)
        ]
        for copy in copies:
            copy.start()

        @pl.when(cycle == 0)
        def finish_setup():
            last = chunk_copy(place, CHUNKS - 1, 0, far)
            last.wait_recv()
            chunk_copy(far_place, CHUNKS - 1, 1, near).start()
            for copy in setup:
                copy.wait()
            wanted = jnp.concatenate(
                [slabs[t, 0, :coarse_own, :FACES] for t in range(tele)], axis=0
            )
            kinds = jnp.concatenate(
                [slabs[t, 1, :coarse_own, :FACES] for t in range(tele)], axis=0
            )
            kinds = flip(kinds.astype(F32))
            coarse_gather[...] = gather_matrix(wanted, fine, columns, coarse)
            kind_masks(kinds, coarse_kinds, coarse)
            near_copy.wait()
            for chunk in range(CHUNKS):
                chunk_copy(place, chunk, 0, far).wait_send()
                chunk_copy(far_place, chunk, 1, near).wait()

        for copy in copies:
            copy.wait()
        total = partials[cycle, 0]
        for j in range(1, tele):
            total = total + partials[cycle, j]
        restricted[...] = flip(total)

        @pl.loop(0, SWEEPS)
        def coarse_body(s):
            @pl.when(s > 0)
            def couple():
                states = exchange(
                    coarse_pool,
                    coarse_send,
                    coarse_recv,
                    cycle * (SWEEPS - 1) + s - 1,
                    column,
                    coarse_state[...],
                )
                coarse_coupled[...] = coupling(states, coarse_gather, coarse_kinds, coarse)

            low = restricted[...]
            low = jnp.where(s > 0, low - coarse_coupled[...], low).astype(BF16)
            coarse_state[...] = apply_inverse(coarse_inverse, low, coarse)

        high, low = split(coarse_state[...])
        state[...] = state[...] + dot(high, member[...]) + dot(low, member[...])

    out_ref[...] = flip(state[...])


def shards(
    fine_size,
    tele,
    right_side,
    fine_inverse,
    fine_links,
    fine_faces,
    coarse_inverse,
    coarse_links,
    coarse_faces,
    face_operators,
    agglomerate,
):
    elements = right_side.shape[0]
    coarse_own = coarse_inverse.shape[0]
    coarse = coarse_own * tele
    types = face_operators.shape[0]
    trace, lift = tables()
    rounds = CYCLES * (SWEEPS + 1)
    coarse_rounds = CYCLES * (SWEEPS - 1)
    vmem = pl.BlockSpec(memory_space=pltpu.VMEM)
    hbm = pl.BlockSpec(memory_space=pltpu.HBM)
    dma = pltpu.SemaphoreType.DMA
    return pl.pallas_call(
        functools.partial(kernel, tele, fine_size),
        out_shape=jax.ShapeDtypeStruct(right_side.shape, F32),
        in_specs=[hbm] * 11,
        out_specs=vmem,
        scratch_shapes=[
            pltpu.VMEM(fine_inverse.shape, BF16),
            pltpu.VMEM(coarse_inverse.shape, BF16),
            pltpu.VMEM((DOFS, elements * DOFS), BF16),
            pltpu.VMEM((tele, DOFS, coarse_own * DOFS), BF16),
            pltpu.VMEM(right_side.shape, F32),
            pltpu.VMEM((FACES, elements), jnp.int32),
            pltpu.VMEM((FACES, elements), jnp.int32),
            pltpu.VMEM(face_operators.shape, BF16),
            pltpu.VMEM(trace.shape, BF16),
            pltpu.VMEM(lift.shape, BF16),
            pltpu.VMEM(coarse_links.shape, jnp.int32),
            pltpu.VMEM(coarse_faces.shape, jnp.int32),
            pltpu.SMEM(agglomerate.shape, jnp.int32),
            pltpu.VMEM((coarse, elements), BF16),
            pltpu.VMEM((tele, 2, 8, LANES), jnp.int32),
            pltpu.VMEM((FACE_DOFS, types * FACE_DOFS), BF16),
            pltpu.VMEM((types * FACE_DOFS, FACES * elements), BF16),
            pltpu.VMEM((types, FACE_DOFS, FACES * elements), BF16),
            pltpu.VMEM((types, FACE_DOFS, FACES * coarse), BF16),
            pltpu.VMEM((FACES * elements, 3 * SLOT), BF16),
            pltpu.VMEM((FACES * coarse, 3 * SLOT), BF16),
            pltpu.VMEM((rounds, 3 * SLOT, DOFS), BF16),
            pltpu.VMEM((coarse_rounds, 3 * SLOT, DOFS), BF16),
            pltpu.VMEM((CYCLES, tele, coarse, DOFS), F32),
            pltpu.VMEM((DOFS, elements), F32),
            pltpu.VMEM((DOFS, elements), F32),
            pltpu.VMEM((DOFS, elements), BF16),
            pltpu.VMEM((DOFS, elements), F32),
            pltpu.VMEM((DOFS, coarse), F32),
            pltpu.VMEM((DOFS, coarse), F32),
            pltpu.VMEM((DOFS, coarse), F32),
            dma((9,)),
            dma((elements,)),
            dma,
            dma,
            dma,
            dma((2, CHUNKS)),
            dma((2, CHUNKS)),
            dma((tele,)),
            dma((tele,)),
            dma((rounds, 2)),
            dma((rounds, 2)),
            dma((coarse_rounds, 2)),
            dma((coarse_rounds, 2)),
            dma((CYCLES, tele)),
            dma((CYCLES, tele)),
        ],
        compiler_params=pltpu.CompilerParams(
            collective_id=0, has_side_effects=True, vmem_limit_bytes=VMEM_BYTES
        ),
        name="v_cycles",
    )(
        right_side,
        fine_inverse,
        fine_links.T,
        fine_faces.T,
        coarse_inverse,
        coarse_links,
        coarse_faces,
        face_operators,
        agglomerate,
        trace,
        lift,
    )


def solution(mesh):
    return jax.shard_map(
        functools.partial(shards, mesh.shape["fine"], mesh.shape["tele"]),
        mesh=mesh,
        in_specs=(
            P(("fine", "tele"), None),
            P(("fine", "tele"), None, None),
            P(("fine", "tele"), None),
            P(("fine", "tele"), None),
            P(("fine", "tele"), None, None),
            P(("fine", "tele"), None),
            P(("fine", "tele"), None),
            P(),
            P(("fine", "tele")),
        ),
        out_specs=P(("fine", "tele"), None),
        check_vma=False,
    )
```

```python
import functools

import jax
import jax.numpy as jnp
import numpy as np
from jax import lax
from jax.experimental import pallas as pl
from jax.experimental.pallas import tpu as pltpu
from jax.sharding import PartitionSpec as P

FIELDS = 5
NODES = 4
SWEEPS = 3
CYCLES = 2
CHUNKS = SWEEPS + 1
FACES = 6
FACE_DOFS = FIELDS * NODES * NODES
DOFS = FIELDS * NODES**3
SLOT = 16
LANES = 128
MAIN = 256
TAIL = DOFS - MAIN
VMEM_BYTES = 60 * 2**20
MESH = pl.DeviceIdType.MESH
F32 = jnp.float32
BF16 = jnp.bfloat16


def face_targets():
    cube = np.arange(DOFS).reshape(FIELDS, NODES, NODES, NODES)
    far = NODES - 1
    slabs = (
        cube[:, 0], cube[:, far], cube[:, :, 0], cube[:, :, far], cube[..., 0], cube[..., far]
    )
    return [slab.reshape(-1) for slab in slabs]


def tables():
    targets = face_targets()
    trace = np.zeros((FACES * FACE_DOFS, DOFS), np.float32)
    lift = np.zeros((DOFS, FACES * FACE_DOFS), np.float32)
    for face in range(FACES):
        rows = face * FACE_DOFS + np.arange(FACE_DOFS)
        trace[rows, targets[face ^ 1]] = 1.0
        lift[targets[face], rows] = 1.0
    return jnp.asarray(trace, BF16), jnp.asarray(lift, BF16)


def dot(a, b):
    return jnp.dot(a, b, preferred_element_type=F32)


def dot_nt(a, b):
    return lax.dot_general(a, b, (((1,), (1,)), ((), ())), preferred_element_type=F32)


def split(value):
    high = value.astype(BF16)
    return high, (value - high.astype(F32)).astype(BF16)


def flip(value):
    rows, columns = value.shape
    pad_rows, pad_columns = -rows % LANES, -columns % LANES
    if pad_columns:
        value = jnp.concatenate([value, jnp.zeros((rows, pad_columns), F32)], axis=1)
    if pad_rows:
        value = jnp.concatenate([value, jnp.zeros((pad_rows, value.shape[1]), F32)], axis=0)
    return value.T[:columns, :rows]


def kernel(
    tele,
    fine_count,
    right_hbm,
    inverse_hbm,
    links_hbm,
    faces_hbm,
    coarse_hbm,
    coarse_links_hbm,
    coarse_faces_hbm,
    operators_hbm,
    agglomerate_hbm,
    trace_hbm,
    lift_hbm,
    out_ref,
    raw,
    coarse_raw,
    inverse,
    coarse_inverse,
    right_in,
    links,
    faces,
    operators_in,
    trace,
    lift,
    coarse_links,
    coarse_faces,
    targets,
    member,
    slabs,
    operators,
    masked,
    fine_kinds,
    coarse_kinds,
    fine_gather,
    coarse_gather,
    fine_pool,
    coarse_pool,
    partials,
    right,
    state,
    lowered,
    coupled,
    restricted,
    coarse_state,
    coarse_coupled,
    load_sem,
    inverse_sem,
    own_sem,
    near_send,
    near_recv,
    block_send,
    block_recv,
    slab_send,
    slab_recv,
    fine_send,
    fine_recv,
    coarse_send,
    coarse_recv,
    sum_send,
    sum_recv,
):
    types = operators_in.shape[0]
    elements = right_in.shape[0]
    coarse_own = coarse_links.shape[0]
    coarse = coarse_own * tele
    fine = lax.axis_index("fine")
    place = lax.axis_index("tele")
    columns = fine_count
    position = fine * tele + place

    def around(offset):
        other = lax.rem(position + offset + columns * tele, columns * tele)
        return (other // tele, lax.rem(other, tele))

    def column(offset):
        return (lax.rem(fine + offset + columns, columns), place)

    def peer(offset):
        return (fine, lax.rem(place + offset, tele))

    pairs = (
        (right_hbm, right_in),
        (links_hbm, links),
        (faces_hbm, faces),
        (operators_hbm, operators_in),
        (trace_hbm, trace),
        (lift_hbm, lift),
        (coarse_links_hbm, coarse_links),
        (coarse_faces_hbm, coarse_faces),
        (agglomerate_hbm, targets),
    )
    loads = [
        pltpu.make_async_copy(source, target, load_sem.at[i])
        for i, (source, target) in enumerate(pairs)
    ]
    own_block = pltpu.make_async_copy(coarse_hbm, coarse_raw, own_sem)
    blocks = [
        pltpu.make_async_copy(inverse_hbm.at[e], raw.at[e], inverse_sem.at[e])
        for e in range(elements)
    ]
    for copy in loads[:1] + blocks + [own_block] + loads[1:]:
        copy.start()

    barrier = pltpu.get_barrier_semaphore()
    partners = [around(1), around(-1), column(1), column(-1)]
    partners += [peer(j) for j in range(1, tele)]
    for partner in partners:
        pl.semaphore_signal(barrier, inc=1, device_id=partner, device_id_type=MESH)

    def gather_matrix(wanted, centre, count, owned):
        lane = lax.broadcasted_iota(jnp.int32, (1, 3 * SLOT), 1)
        target = jnp.full((1, 3 * SLOT), -2, jnp.int32)
        for slot in range(3):
            owner = lax.rem(centre + slot - 1 + count, count)
            inside = (lane >= slot * SLOT) & (lane < slot * SLOT + owned)
            target = jnp.where(inside, owner * owned + lane - slot * SLOT, target)
        return jnp.concatenate(
            [(wanted[:, face : face + 1] == target).astype(F32) for face in range(FACES)], axis=0
        ).astype(BF16)

    def kind_masks(turned, target, width):
        row = jnp.concatenate([turned[face : face + 1] for face in range(FACES)], axis=1)
        for kind in range(types):
            chosen = (row == float(kind)).astype(F32)
            target[kind] = jnp.broadcast_to(chosen, (FACE_DOFS, FACES * width)).astype(BF16)

    coupled[...] = jnp.zeros_like(coupled)
    coarse_coupled[...] = jnp.zeros_like(coarse_coupled)

    pl.semaphore_wait(barrier, len(partners))

    setup = [
        pltpu.make_async_remote_copy(
            src_ref=slabs.at[place],
            dst_ref=slabs.at[place],
            send_sem=slab_send.at[j],
            recv_sem=slab_recv.at[j],
            device_id=peer(j),
            device_id_type=MESH,
        )
        for j in range(1, tele)
    ]

    near = (fine, place + 1 - 2 * lax.rem(place, 2))
    far_place = lax.rem(place + 2, tele)
    far = (fine, far_place)
    chunk_rows = DOFS // CHUNKS

    def pack_own():
        own_block.wait()
        coarse_inverse[place, :, :MAIN] = coarse_raw[0, :, :MAIN]
        coarse_inverse[place, :, MAIN : 2 * MAIN] = coarse_raw[1, :, :MAIN]
        coarse_inverse[place, :, 2 * MAIN :] = jnp.concatenate(
            [coarse_raw[0, :, MAIN:], coarse_raw[1, :, MAIN:]], axis=1
        )

    def chunk_copy(owner, chunk, leg, device):
        part = coarse_inverse.at[owner, pl.ds(pl.multiple_of(chunk * chunk_rows, 16), chunk_rows)]
        return pltpu.make_async_remote_copy(
            src_ref=part,
            dst_ref=part,
            send_sem=block_send.at[leg, chunk],
            recv_sem=block_recv.at[leg, chunk],
            device_id=device,
            device_id_type=MESH,
        )

    near_copy = pltpu.make_async_remote_copy(
        src_ref=coarse_inverse.at[place],
        dst_ref=coarse_inverse.at[place],
        send_sem=near_send,
        recv_sem=near_recv,
        device_id=near,
        device_id_type=MESH,
    )
    def fine_tables():
        for copy in loads[1:]:
            copy.wait()
        operators[...] = jnp.concatenate([operators_in[kind] for kind in range(types)], axis=1)
        wanted = flip(links[...].astype(F32)).astype(jnp.int32)
        fine_gather[...] = gather_matrix(wanted, position, columns * tele, elements)
        kind_masks(faces[...].astype(F32), fine_kinds, elements)
        slabs[place, 0, :coarse_own, :FACES] = coarse_links[...]
        slabs[place, 1, :coarse_own, :FACES] = coarse_faces[...]
        for copy in setup:
            copy.start()
        lane = lax.broadcasted_iota(jnp.int32, (coarse, elements), 1)
        target = jnp.zeros((coarse, elements), jnp.int32)
        for e in range(elements):
            target = jnp.where(lane == e, targets[e], target)
        row = lax.broadcasted_iota(jnp.int32, (coarse, elements), 0)
        member[...] = (target == row + fine * coarse).astype(F32).astype(BF16)

    def pack(source, target, e):
        target[:, e * MAIN : (e + 1) * MAIN] = source[e, :, :MAIN]
        if e % 2:
            at = source.shape[0] * MAIN + (e - 1) * TAIL
            target[:, at : at + 2 * TAIL] = jnp.concatenate(
                [source[e - 1, :, MAIN:], source[e, :, MAIN:]], axis=1
            )

    def apply_inverse(packed, vectors, width):
        lane = lax.broadcasted_iota(jnp.int32, (1, width), 1)
        alone = [vectors * (lane == e).astype(F32).astype(BF16) for e in range(width)]
        group = width // len(packed)
        total = None
        for i, block in enumerate(packed):
            own = alone[i * group : (i + 1) * group]
            spread = jnp.concatenate(
                [part[:MAIN] for part in own] + [part[MAIN:] for part in own], axis=0
            )
            product = dot(block, spread)
            total = product if total is None else total + product
        return total

    def sides(pool, send, recv, step, partner):
        return [
            pltpu.make_async_remote_copy(
                src_ref=pool.at[step, pl.ds(SLOT, SLOT)],
                dst_ref=pool.at[step, pl.ds(landing * SLOT, SLOT)],
                send_sem=send.at[step, side],
                recv_sem=recv.at[step, side],
                device_id=partner(offset),
                device_id_type=MESH,
            )
            for side, (offset, landing) in enumerate(((1, 0), (-1, 2)))
        ]

    def exchange(pool, send, recv, step, partner, value, meanwhile=lambda: None):
        rows = flip(value)
        if rows.shape[0] < SLOT:
            rows = jnp.concatenate(
                [rows, jnp.zeros((SLOT - rows.shape[0], DOFS), F32)], axis=0
            )
        pool[step, SLOT : 2 * SLOT, :] = rows.astype(BF16)
        copies = sides(pool, send, recv, step, partner)
        for copy in copies:
            copy.start()
        meanwhile()
        for copy in copies:
            copy.wait_recv()
        return pool[step]

    def coupling(states, gather, kinds, width):
        picked = dot(gather[...], states).astype(BF16)
        traces = dot_nt(trace[...], picked)
        span = FACES * width
        lane = lax.broadcasted_iota(jnp.int32, (FACE_DOFS, span), 1)
        rows = traces[:FACE_DOFS]
        for face in range(1, FACES):
            rows = jnp.where(
                lane >= face * width, traces[face * FACE_DOFS : (face + 1) * FACE_DOFS], rows
            )
        rows = rows.astype(BF16)
        for kind in range(types):
            masked[kind * FACE_DOFS : (kind + 1) * FACE_DOFS, :span] = rows * kinds[kind]
        products = dot(operators[...], masked[:, :span]).astype(BF16)
        stacked = jnp.concatenate(
            [products[:, face * width : (face + 1) * width] for face in range(FACES)], axis=0
        )
        return dot(lift[...], stacked)

    loads[0].wait()
    right[...] = flip(right_in[...])
    for e in range(elements):
        blocks[e].wait()
        pack(raw, inverse, e)

    pack_own()
    near_copy.start()
    chunk_copy(place, 0, 0, far).start()

    @pl.loop(0, CYCLES)
    def cycle_body(cycle):
        @pl.loop(0, SWEEPS + 1)
        def sweep_body(s):
            @pl.when(cycle + s > 0)
            def couple():
                def meanwhile():
                    pl.when(cycle * (SWEEPS + 1) + s == 1)(fine_tables)

                states = exchange(
                    fine_pool,
                    fine_send,
                    fine_recv,
                    cycle * (SWEEPS + 1) + s,
                    around,
                    state[...],
                    meanwhile,
                )

                @pl.when(cycle == 0)
                def pass_on():
                    chunk_copy(place, s - 1, 0, far).wait_recv()
                    chunk_copy(far_place, s - 1, 1, near).start()
                    chunk_copy(place, s, 0, far).start()

                coupled[...] = coupling(states, fine_gather, fine_kinds, elements)

            @pl.when(s < SWEEPS)
            def relax():
                low = (right[...] - coupled[...]).astype(BF16)
                lowered[...] = low
                state[...] = apply_inverse([inverse[...]], low, elements)

        high, low = split(lowered[...].astype(F32) - coupled[...])
        partials[cycle, 0] = dot_nt(member[...], high) + dot_nt(member[...], low)
        copies = [
            pltpu.make_async_remote_copy(
                src_ref=partials.at[cycle, 0],
                dst_ref=partials.at[cycle, j],
                send_sem=sum_send.at[cycle, j],
                recv_sem=sum_recv.at[cycle, j],
                device_id=peer(j),
                device_id_type=MESH,
            )
            for j in range(1, tele)
        ]
        for copy in copies:
            copy.start()

        @pl.when(cycle == 0)
        def finish_setup():
            last = chunk_copy(place, CHUNKS - 1, 0, far)
            last.wait_recv()
            chunk_copy(far_place, CHUNKS - 1, 1, near).start()
            for copy in setup:
                copy.wait()
            wanted = jnp.concatenate(
                [slabs[t, 0, :coarse_own, :FACES] for t in range(tele)], axis=0
            )
            kinds = jnp.concatenate(
                [slabs[t, 1, :coarse_own, :FACES] for t in range(tele)], axis=0
            )
            kinds = flip(kinds.astype(F32))
            coarse_gather[...] = gather_matrix(wanted, fine, columns, coarse)
            kind_masks(kinds, coarse_kinds, coarse)
            near_copy.wait()
            for chunk in range(CHUNKS):
                chunk_copy(place, chunk, 0, far).wait_send()
                chunk_copy(far_place, chunk, 1, near).wait()

        for copy in copies:
            copy.wait()
        total = partials[cycle, 0]
        for j in range(1, tele):
            total = total + partials[cycle, j]
        restricted[...] = flip(total)

        @pl.loop(0, SWEEPS)
        def coarse_body(s):
            @pl.when(s > 0)
            def couple():
                states = exchange(
                    coarse_pool,
                    coarse_send,
                    coarse_recv,
                    cycle * (SWEEPS - 1) + s - 1,
                    column,
                    coarse_state[...],
                )
                coarse_coupled[...] = coupling(states, coarse_gather, coarse_kinds, coarse)

            low = restricted[...]
            low = jnp.where(s > 0, low - coarse_coupled[...], low).astype(BF16)
            coarse_state[...] = apply_inverse([coarse_inverse[t] for t in range(tele)], low, coarse)

        high, low = split(coarse_state[...])
        state[...] = state[...] + dot(high, member[...]) + dot(low, member[...])

    out_ref[...] = flip(state[...])
    for step in range(1, fine_pool.shape[0]):
        for copy in sides(fine_pool, fine_send, fine_recv, step, around):
            copy.wait_send()
    for step in range(coarse_pool.shape[0]):
        for copy in sides(coarse_pool, coarse_send, coarse_recv, step, column):
            copy.wait_send()


def shards(
    fine_size,
    tele,
    right_side,
    fine_inverse,
    fine_links,
    fine_faces,
    coarse_inverse,
    coarse_links,
    coarse_faces,
    face_operators,
    agglomerate,
):
    elements = right_side.shape[0]
    coarse_own = coarse_inverse.shape[0]
    coarse = coarse_own * tele
    types = face_operators.shape[0]
    trace, lift = tables()
    rounds = CYCLES * (SWEEPS + 1)
    coarse_rounds = CYCLES * (SWEEPS - 1)
    vmem = pl.BlockSpec(memory_space=pltpu.VMEM)
    hbm = pl.BlockSpec(memory_space=pltpu.HBM)
    dma = pltpu.SemaphoreType.DMA
    return pl.pallas_call(
        functools.partial(kernel, tele, fine_size),
        out_shape=jax.ShapeDtypeStruct(right_side.shape, F32),
        in_specs=[hbm] * 11,
        out_specs=vmem,
        scratch_shapes=[
            pltpu.VMEM(fine_inverse.shape, BF16),
            pltpu.VMEM(coarse_inverse.shape, BF16),
            pltpu.VMEM((DOFS, elements * DOFS), BF16),
            pltpu.VMEM((tele, DOFS, coarse_own * DOFS), BF16),
            pltpu.VMEM(right_side.shape, F32),
            pltpu.VMEM((FACES, elements), jnp.int32),
            pltpu.VMEM((FACES, elements), jnp.int32),
            pltpu.VMEM(face_operators.shape, BF16),
            pltpu.VMEM(trace.shape, BF16),
            pltpu.VMEM(lift.shape, BF16),
            pltpu.VMEM(coarse_links.shape, jnp.int32),
            pltpu.VMEM(coarse_faces.shape, jnp.int32),
            pltpu.SMEM(agglomerate.shape, jnp.int32),
            pltpu.VMEM((coarse, elements), BF16),
            pltpu.VMEM((tele, 2, 8, LANES), jnp.int32),
            pltpu.VMEM((FACE_DOFS, types * FACE_DOFS), BF16),
            pltpu.VMEM((types * FACE_DOFS, FACES * elements), BF16),
            pltpu.VMEM((types, FACE_DOFS, FACES * elements), BF16),
            pltpu.VMEM((types, FACE_DOFS, FACES * coarse), BF16),
            pltpu.VMEM((FACES * elements, 3 * SLOT), BF16),
            pltpu.VMEM((FACES * coarse, 3 * SLOT), BF16),
            pltpu.VMEM((rounds, 3 * SLOT, DOFS), BF16),
            pltpu.VMEM((coarse_rounds, 3 * SLOT, DOFS), BF16),
            pltpu.VMEM((CYCLES, tele, coarse, DOFS), F32),
            pltpu.VMEM((DOFS, elements), F32),
            pltpu.VMEM((DOFS, elements), F32),
            pltpu.VMEM((DOFS, elements), BF16),
            pltpu.VMEM((DOFS, elements), F32),
            pltpu.VMEM((DOFS, coarse), F32),
            pltpu.VMEM((DOFS, coarse), F32),
            pltpu.VMEM((DOFS, coarse), F32),
            dma((9,)),
            dma((elements,)),
            dma,
            dma,
            dma,
            dma((2, CHUNKS)),
            dma((2, CHUNKS)),
            dma((tele,)),
            dma((tele,)),
            dma((rounds, 2)),
            dma((rounds, 2)),
            dma((coarse_rounds, 2)),
            dma((coarse_rounds, 2)),
            dma((CYCLES, tele)),
            dma((CYCLES, tele)),
        ],
        compiler_params=pltpu.CompilerParams(
            collective_id=0, has_side_effects=True, vmem_limit_bytes=VMEM_BYTES
        ),
        name="v_cycles",
    )(
        right_side,
        fine_inverse,
        fine_links.T,
        fine_faces.T,
        coarse_inverse,
        coarse_links,
        coarse_faces,
        face_operators,
        agglomerate,
        trace,
        lift,
    )


def solution(mesh):
    return jax.shard_map(
        functools.partial(shards, mesh.shape["fine"], mesh.shape["tele"]),
        mesh=mesh,
        in_specs=(
            P(("fine", "tele"), None),
            P(("fine", "tele"), None, None),
            P(("fine", "tele"), None),
            P(("fine", "tele"), None),
            P(("fine", "tele"), None, None),
            P(("fine", "tele"), None),
            P(("fine", "tele"), None),
            P(),
            P(("fine", "tele")),
        ),
        out_specs=P(("fine", "tele"), None),
        check_vma=False,
    )
```
